512 devices in a mesh: node: 32 (over x, z_lo), local: 16 (over z_hi, y, core).
Axes of the slice: x: 4, y: 4, z: 16 (z_hi: 2, z_lo: 8; z = z_hi * 8 + z_lo), core: 2. Of those that a mesh axis runs over, the one named last changes fastest.
Arguments:
- acts: bfloat16 [114688, 4096], P(('node', 'local')), may hold values from -24 to 24
- grads_out: bfloat16 [114688, 1024], P(('node', 'local')), may hold values from -6 to 6
- quant: bfloat16 [4096, 1024], P('local'), may hold values from -127 to 127, as said below
- scales: float32 [4096, 8], P('local'), may hold values from 5e-05 to 0.0005
Outputs:
- grad_input: bfloat16 [114688, 4096], P(('node', 'local'))
- weight_grad: float32 [4096, 1024], P(('local', 'node'))
The draws below stay inside these ranges and needn't reach their ends.
Inputs may be any that keep to these rules, and one draw needn't show every extreme that they name: quant holds whole numbers.
All inputs are finite; a program needn't handle non-finite values.
Results may differ from the reference program's by a relative error of at most 0.0049.
Values may be sent and summed in bfloat16 or wider, within the bound.
No kernel may reach another device: no remote copies, remote signals or barrier semaphores. Data moves between devices by JAX's collectives and lax.ppermute only.
A program may use at most 128 MiB of HBM per device.

```python
import math
import jax
import jax.numpy as jnp
from jax import lax

D = 4096
KV = 1024
BLOCK = 128
TOK_DEV = 224
TOKENS = 114688
N_NODE = 32
N_LOCAL = 16


def draw_quant(key, part):
    key = jax.random.fold_in(key, 7)
    levels = jax.random.randint(key, (D, KV), -127, 128)
    return levels.astype(jnp.float32).astype(jnp.bfloat16)


def with_spikes(array, rng, source, target, blocks, factor):
    def block_of(dim):
        return (jnp.arange(array.shape[dim]) // (array.shape[dim] // blocks)).reshape((-1,) + (1,) * (array.ndim - 1 - dim))

    first = jax.random.permutation(rng, blocks)[block_of(target)]
    second = (block_of(target) + blocks // 2) % blocks
    return jnp.where((block_of(source) == first) | (block_of(source) == second), factor * array, array)


def level_of(stream_key, dims, pieces, least, largest):
    gain = 1.0
    for dim, blocks in pieces:
        heights = jax.random.uniform(jax.random.fold_in(jax.random.fold_in(stream_key, 6), dim), (blocks,), jnp.float32, least / len(pieces), largest / len(pieces))
        gain = gain * jnp.repeat(jnp.exp(heights), dims[dim] // blocks).reshape((-1,) + (1,) * (len(dims) - 1 - dim))
    return gain


def centred(rng, shape, spread, most, cuts=(), kind=jnp.bfloat16):
    loudness = level_of(rng, shape, cuts, -0.22, 0.18) if cuts else 1.0
    entries = jax.random.normal(rng, shape, jnp.float32) * spread * loudness
    return jnp.minimum(jnp.maximum(entries, -most), most).astype(kind)


def noise_with(key, extent, width, limit, cuts, heavy, kind=jnp.bfloat16):
    entries = width * jax.random.normal(key, extent, jnp.float32)
    if cuts:
        entries = entries * level_of(key, extent, cuts, -0.22, 0.18)
    return jnp.clip(with_spikes(entries, jax.random.fold_in(key, 3), *heavy), -limit, limit).astype(kind)


def setup_inputs(seed: int = 0) -> dict:
    keys = jax.random.split(jax.random.key(seed), 5)
    acts = noise_with(keys[0], (TOKENS, D), 1.0, 24.0, ((0, 512),), (0, 1, 512, 6.0))
    grads_out = centred(keys[1], (TOKENS, KV), 1.0, 6.0, ((0, 512),))
    quant = draw_quant(jax.random.fold_in(keys[4], 71), 0)
    scales = jnp.clip(jnp.exp(math.log(0.0005) - 2.3025852 * jax.random.uniform(keys[3], (D, KV // BLOCK), jnp.float32) ** level_of(keys[3], (D, KV // BLOCK), ((0, 16),), -0.2, 0.2)), 4.999999873689376e-05, 0.0005)
    return dict(acts=acts, grads_out=grads_out, quant=quant, scales=scales)


def reference(acts, grads_out, quant, scales):
    weight = (quant.astype(jnp.float32).reshape(D, KV // BLOCK, BLOCK) * scales[:, :, None]).reshape(D, KV).astype(jnp.bfloat16)
    grad_input = lax.dot_general(grads_out, weight, (((1,), (1,)), ((), ())), preferred_element_type=jnp.float32).astype(jnp.bfloat16)
    factor = 1.0 / math.sqrt(TOKENS)
    acts_blocks = acts.reshape(N_NODE, N_LOCAL, TOK_DEV, D)
    grads_blocks = grads_out.reshape(N_NODE, N_LOCAL, TOK_DEV, KV)

    def device_term(total, pair):
        inputs, outputs = pair
        part = lax.dot_general(inputs, outputs, (((0,), (0,)), ((), ())), preferred_element_type=jnp.float32)
        part = lax.optimization_barrier((part * factor).astype(jnp.bfloat16))
        return (total + part.astype(jnp.float32), None)

    def group_term(total, pair):
        inner, _ = lax.scan(device_term, jnp.zeros((D, KV), jnp.float32), pair)
        rounded = lax.optimization_barrier(inner.astype(jnp.bfloat16))
        return (total + rounded.astype(jnp.float32), None)
    weight_grad, _ = lax.scan(group_term, jnp.zeros((D, KV), jnp.float32), (acts_blocks, grads_blocks))
    return (grad_input, weight_grad)
```

```python
import math

import jax
import jax.numpy as jnp
from jax import lax
from jax.sharding import Mesh
from jax.sharding import PartitionSpec as P

BLOCK = 128
NX, NZL, NZH, NY, NC = 4, 8, 2, 4, 2
NZ = NZL * NZH
AXES = ("x", "zl", "zh", "y", "c")


def shift(value, axis, step):
    size = lax.axis_size(axis)
    return lax.ppermute(value, axis, [(i, (i + step) % size) for i in range(size)])


def chip_shift(value, move):
    def index(x, z, y, c):
        return (((x * NZL + z % NZL) * NZH + z // NZL) * NY + y) * NC + c

    pairs = [
        (index(x, z, y, c), index(x, move(z), y, c))
        for x in range(NX)
        for z in range(NZ)
        for y in range(NY)
        for c in range(NC)
    ]
    return lax.ppermute(value, AXES, pairs)


def pick(array, index, axis):
    return lax.dynamic_index_in_dim(array, index, axis, keepdims=False)


def total_of(parts):
    total = parts[0].astype(jnp.float32)
    for part in parts[1:]:
        total = total + part.astype(jnp.float32)
    return total


def shards(acts, grads_out, quant, scales):
    tokens, width = acts.shape
    columns = grads_out.shape[1]
    shard_rows = quant.shape[0]
    total_tokens = tokens * lax.axis_size(AXES)
    x, zl, zh, y, c = (lax.axis_index(name) for name in AXES)
    z = zh * NZL + zl
    bf16 = jnp.bfloat16

    blocked = (
        quant.astype(jnp.float32).reshape(shard_rows, columns // BLOCK, BLOCK) * scales[:, :, None]
    )
    weight = blocked.reshape(shard_rows, columns).astype(bf16)

    quarter = lax.dynamic_slice_in_dim(weight, x * (shard_rows // NX), shard_rows // NX, 0)
    other = chip_shift(quarter, lambda i: (i + NZL) % NZ)
    own_half = lax.all_gather(weight, ("y", "c"), axis=0, tiled=True)
    other_half = lax.all_gather(other, ("x", "y", "c"), axis=0, tiled=True)
    other_half = (
        other_half.reshape(NX, NY * NC, shard_rows // NX, columns)
        .transpose(1, 0, 2, 3)
        .reshape(NY * NC * shard_rows, columns)
    )

    groups = acts.reshape(tokens, NZH * NY, NC, width // (NZH * NY * NC))
    mine = pick(groups, c, 2).reshape(tokens, width // NC)
    theirs = pick(groups, 1 - c, 2).reshape(tokens, width // NC)
    acts_in = shift(theirs, "c", 1)
    grads_in = shift(grads_out, "c", 1)
    acts_two = jnp.concatenate([mine, acts_in], axis=0)
    grads_two = jnp.concatenate([grads_out, grads_in], axis=0)
    factor = 1.0 / math.sqrt(total_tokens)
    part = lax.dot_general(
        acts_two, grads_two, (((0,), (0,)), ((), ())), preferred_element_type=jnp.float32
    )
    part = (part * factor).astype(bf16)
    half = columns // 2
    part = part.reshape(NZH, NY, NX, NZL * 8, columns)

    left, right = part[..., :half], part[..., half:]
    left_in, right_in = [pick(left, y, 1)], [pick(right, x, 2)]
    for k in (1, 3, 2):
        left_in.append(shift(pick(left, (y + k) % NY, 1), "y", k))
        right_in.append(shift(pick(right, (x + k) % NX, 2), "x", k))
    left = total_of(left_in).astype(bf16)
    right = total_of(right_in).astype(bf16)
    left_in, right_in = [pick(left, x, 1)], [pick(right, y, 1)]
    for k in (1, 3, 2):
        left_in.append(shift(pick(left, (x + k) % NX, 1), "x", k))
        right_in.append(shift(pick(right, (y + k) % NY, 1), "y", k))
    left, right = total_of(left_in), total_of(right_in)
    rows = jnp.concatenate([left, right], axis=-1).astype(bf16)
    rows = rows.reshape(4, 4, 8, columns)
    run, place = z // 4, z % 4
    parts = [pick(rows, place, 1)]
    for k in (1, 3, 2):
        parts.append(
            chip_shift(
                pick(rows, (place + k) % 4, 1),
                lambda i, k=k: (i // 4) * 4 + (i + k) % 4,
            )
        )
    rows = total_of(parts)
    parts = [pick(rows, run, 0)]
    for k in (1, 3, 2):
        parts.append(chip_shift(pick(rows, (run + k) % 4, 0), lambda i, k=k: (i + 4 * k) % NZ))
    weight_grad = total_of(parts)

    def input_half(rows_half):
        return lax.dot_general(
            grads_out, rows_half, (((1,), (1,)), ((), ())), preferred_element_type=jnp.float32
        ).astype(bf16)

    own, far = input_half(own_half), input_half(other_half)
    low, high = jnp.where(zh == 0, own, far), jnp.where(zh == 0, far, own)
    grad_input = jnp.concatenate([low, high], axis=1)
    return (grad_input, weight_grad)


def solution(mesh):
    fine = Mesh(mesh.devices.reshape(NX, NZL, NZH, NY, NC), AXES)
    tokens = P(AXES, None)
    rows = P(("zh", "y", "c"), None)
    return jax.shard_map(
        shards,
        mesh=fine,
        in_specs=(tokens, tokens, rows, rows),
        out_specs=(tokens, P(("zh", "y", "c", "x", "zl"), None)),
        check_vma=False,
    )
```

```python
import functools
import math

import jax
import jax.numpy as jnp
from jax import lax
from jax.experimental import pallas as pl
from jax.experimental.pallas import tpu as pltpu
from jax.sharding import Mesh
from jax.sharding import PartitionSpec as P

BLOCK = 128
NX, NZL, NZH, NY, NC = 4, 8, 2, 4, 2
NZ = NZL * NZH
AXES = ("x", "zl", "zh", "y", "c")
VMEM_LIMIT = 40 * 1024 * 1024


def shift(value, axis, step):
    size = lax.axis_size(axis)
    return lax.ppermute(value, axis, [(i, (i + step) % size) for i in range(size)])


def chip_shift(value, move):
    def index(x, z, y, c):
        return (((x * NZL + z % NZL) * NZH + z // NZL) * NY + y) * NC + c

    pairs = []
    for x in range(NX):
        for z in range(NZ):
            to_x, to_z = move(x, z)
            for y in range(NY):
                for c in range(NC):
                    pairs.append((index(x, z, y, c), index(to_x, to_z, y, c)))
    return lax.ppermute(value, AXES, pairs)


def pick(array, index, axis):
    return lax.dynamic_index_in_dim(array, index, axis, keepdims=False)


def total_of(parts):
    total = parts[0].astype(jnp.float32)
    for part in parts[1:]:
        total = total + part.astype(jnp.float32)
    return total


def partial_kernel(factor, where, acts, acts_in, grads, grads_in, o0, o1, o2, o3, total):
    dims = (((0,), (0,)), ((), ()))
    value = lax.dot_general(acts[...], grads[...], dims, preferred_element_type=jnp.float32)
    value += lax.dot_general(acts_in[...], grads_in[...], dims, preferred_element_type=jnp.float32)
    total[...] = value * factor
    rows = total.shape[0] // NX
    for k, out in enumerate((o0, o1, o2, o3)):
        start = pl.multiple_of(lax.rem(where[1] + k, NX) * rows, rows)
        out[0] = total[pl.ds(start, rows), :].astype(out.dtype)


def partials(where, acts, acts_in, grads, grads_in, factor):
    tokens, width = acts.shape
    columns = grads.shape[1]
    blocks = NZH * NY
    own = width // (blocks * NC)
    rows = own // NX
    acts_spec = pl.BlockSpec((tokens, own), lambda j, where: (0, j * NC + where[0]))
    grads_spec = pl.BlockSpec((tokens, columns), lambda j, where: (0, 0))
    out_spec = pl.BlockSpec(
        (1, rows, columns),
        lambda j, where: (lax.rem(j % NY + NY - where[2], NY) * NZH + j // NY, 0, 0),
    )
    return pl.pallas_call(
        functools.partial(partial_kernel, factor),
        out_shape=[jax.ShapeDtypeStruct((blocks, rows, columns), jnp.bfloat16)] * NX,
        grid_spec=pltpu.PrefetchScalarGridSpec(
            num_scalar_prefetch=1,
            grid=(blocks,),
            in_specs=[acts_spec, acts_spec, grads_spec, grads_spec],
            out_specs=[out_spec] * NX,
            scratch_shapes=[pltpu.VMEM((own, columns), jnp.float32)],
        ),
        compiler_params=pltpu.CompilerParams(vmem_limit_bytes=VMEM_LIMIT),
        cost_estimate=pl.CostEstimate(
            flops=4 * tokens * columns * own * blocks,
            bytes_accessed=2 * blocks * own * columns + 4 * tokens * width,
            transcendentals=0,
        ),
        name="partials",
    )(where, acts, acts_in, grads, grads_in)


def input_kernel(where, grads, weight, *rest):
    out = rest[-1]
    out[...] = lax.dot_general(
        grads[...], weight[...], (((1,), (1,)), ((), ())), preferred_element_type=jnp.float32
    ).astype(out.dtype)


def input_half(where, grads, weight, width, before=None):
    tokens, columns = grads.shape
    rows = weight.shape[0]
    steps = 4
    block = rows // steps
    in_specs = [
        pl.BlockSpec((tokens, columns), lambda j, where: (0, 0)),
        pl.BlockSpec((block, columns), lambda j, where: (j, 0)),
    ]
    args = [where, grads, weight]
    aliases = {}
    if before is not None:
        in_specs.append(pl.BlockSpec(memory_space=pl.ANY))
        args.append(before)
        aliases = {3: 0}
    return pl.pallas_call(
        input_kernel,
        out_shape=jax.ShapeDtypeStruct((tokens, width), jnp.bfloat16),
        grid_spec=pltpu.PrefetchScalarGridSpec(
            num_scalar_prefetch=1,
            grid=(steps,),
            in_specs=in_specs,
            out_specs=pl.BlockSpec((tokens, block), lambda j, where: (0, where[0] * steps + j)),
        ),
        input_output_aliases=aliases,
        compiler_params=pltpu.CompilerParams(vmem_limit_bytes=VMEM_LIMIT),
        cost_estimate=pl.CostEstimate(
            flops=2 * tokens * columns * rows,
            bytes_accessed=2 * rows * columns + 2 * tokens * (columns + rows),
            transcendentals=0,
        ),
        name="input_half",
    )(*args)


def shards(acts, grads_out, quant, scales):
    tokens, width = acts.shape
    columns = grads_out.shape[1]
    shard_rows = quant.shape[0]
    total_tokens = tokens * lax.axis_size(AXES)
    x, zl, zh, y, c = (lax.axis_index(name) for name in AXES)
    bf16 = jnp.bfloat16

    acts_in = shift(acts, "c", 1)
    grads_in = shift(grads_out, "c", 1)

    blocked = (
        quant.astype(jnp.float32).reshape(shard_rows, columns // BLOCK, BLOCK) * scales[:, :, None]
    )
    weight = blocked.reshape(shard_rows, columns).astype(bf16)
    own_half = lax.all_gather(weight, ("y", "c"), axis=0, tiled=True)

    far = chip_shift(weight, lambda i, z: (i, (z + NZL) % NZ))

    where = jnp.stack([c, x, y]).astype(jnp.int32)
    parts = partials(where, acts, acts_in, grads_out, grads_in, 1.0 / math.sqrt(total_tokens))

    parts = [part.reshape(NY, NZH * NZL * 8, columns) for part in parts]
    received = [parts[0]] + [shift(parts[k], "x", k) for k in (1, 3, 2)]
    own = input_half(zh[None].astype(jnp.int32), grads_out, own_half, width)
    far, own, *received = lax.optimization_barrier((far, own, *received))
    other_half = lax.all_gather(far, ("y", "c"), axis=0, tiled=True)
    summed = [total_of([part[k] for part in received]).astype(bf16) for k in range(NY)]
    received = [summed[0]] + [shift(summed[k], "y", k) for k in (1, 3, 2)]
    rows = total_of(received).astype(bf16).reshape(NZ, 8, columns)
    rows = lax.all_to_all(rows, ("zh", "zl"), split_axis=0, concat_axis=0, tiled=True)
    grad_input = input_half((1 - zh)[None].astype(jnp.int32), grads_out, other_half, width, own)
    rows, grad_input = lax.optimization_barrier((rows, grad_input))
    weight_grad = jnp.sum(rows, axis=0, dtype=jnp.float32)
    return (grad_input, weight_grad)


def solution(mesh):
    fine = Mesh(mesh.devices.reshape(NX, NZL, NZH, NY, NC), AXES)
    tokens = P(AXES, None)
    rows = P(("zh", "y", "c"), None)
    return jax.shard_map(
        shards,
        mesh=fine,
        in_specs=(tokens, tokens, rows, rows),
        out_specs=(tokens, P(("zh", "y", "c", "x", "zl"), None)),
        check_vma=False,
    )
```

```python
import functools
import math

import jax
import jax.numpy as jnp
from jax import lax
from jax.experimental import pallas as pl
from jax.experimental.pallas import tpu as pltpu
from jax.sharding import Mesh
from jax.sharding import PartitionSpec as P

BLOCK = 128
NX, NZL, NZH, NY, NC = 4, 8, 2, 4, 2
NZ = NZL * NZH
AXES = ("x", "zl", "zh", "y", "c")
VMEM_LIMIT = 40 * 1024 * 1024


def shift(value, axis, step):
    size = lax.axis_size(axis)
    return lax.ppermute(value, axis, [(i, (i + step) % size) for i in range(size)])


def chip_shift(value, move):
    def index(x, z, y, c):
        return (((x * NZL + z % NZL) * NZH + z // NZL) * NY + y) * NC + c

    pairs = []
    for x in range(NX):
        for z in range(NZ):
            to_x, to_z = move(x, z)
            for y in range(NY):
                for c in range(NC):
                    pairs.append((index(x, z, y, c), index(to_x, to_z, y, c)))
    return lax.ppermute(value, AXES, pairs)


def pick(array, index, axis):
    return lax.dynamic_index_in_dim(array, index, axis, keepdims=False)


def total_of(parts):
    total = parts[0].astype(jnp.float32)
    for part in parts[1:]:
        total = total + part.astype(jnp.float32)
    return total


def weight_kernel(where, quant, scales, weight, quarter):
    rows, columns = quant.shape
    levels = quant[...].astype(jnp.float32)
    factors = scales[...].T
    for block in range(columns // BLOCK):
        run = slice(block * BLOCK, (block + 1) * BLOCK)
        weight[:, run] = (levels[:, run] * factors[:, block : block + 1]).astype(weight.dtype)
    part = quarter.shape[0]
    quarter[...] = weight[pl.ds(pl.multiple_of(where[1] * part, part), part), :]


def weights(where, quant, scales):
    rows, columns = quant.shape
    vmem = pl.BlockSpec(memory_space=pltpu.VMEM)
    return pl.pallas_call(
        weight_kernel,
        out_shape=[
            jax.ShapeDtypeStruct((rows, columns), jnp.bfloat16),
            jax.ShapeDtypeStruct((rows // NX, columns), jnp.bfloat16),
        ],
        in_specs=[pl.BlockSpec(memory_space=pltpu.SMEM), vmem, vmem],
        out_specs=[vmem, vmem],
        compiler_params=pltpu.CompilerParams(vmem_limit_bytes=VMEM_LIMIT),
        cost_estimate=pl.CostEstimate(
            flops=rows * columns, bytes_accessed=4 * rows * columns, transcendentals=0
        ),
        name="weights",
    )(where, quant, scales.T)


def partial_kernel(
    factor, where, acts, acts_in, grads, grads_in, own, right, left, far_a, far_b, lhs, rhs
):
    step = pl.program_id(0)
    tokens = acts.shape[0]
    blocks, rows, _ = own.shape
    span = rows * NX

    @pl.when(step == 0)
    def _():
        rhs[:tokens] = grads[...]
        rhs[tokens:] = grads_in[...]

    for t in range(blocks):
        j = step * blocks + t
        block = (j % NZH) * NY + lax.rem(where[2] + j // NZH, NY)
        start = pl.multiple_of((block * NC + where[0]) * span, span)
        lhs[:tokens, t * span : (t + 1) * span] = acts[:, pl.ds(start, span)]
        lhs[tokens:, t * span : (t + 1) * span] = acts_in[:, pl.ds(start, span)]
    value = lax.dot_general(
        lhs[...], rhs[...], (((0,), (0,)), ((), ())), preferred_element_type=jnp.float32
    )
    value = (value * factor).astype(own.dtype)

    def chunk(x, t, k):
        start = t * span + (x + k) % NX * rows
        return value[start : start + rows]

    for x in range(NX):

        @pl.when(where[1] == x)
        def _():
            for t in range(blocks):
                own[t] = chunk(x, t, 0)
                right[t] = chunk(x, t, 1)
                left[t] = chunk(x, t, 3)

            @pl.when(step == 0)
            def _():
                for t in range(blocks):
                    far_a[t] = chunk(x, t, 2)

            @pl.when(step == 1)
            def _():
                for t in range(blocks):
                    far_b[t] = chunk(x, t, 2)


def partials(where, acts, acts_in, grads, grads_in, factor):
    tokens, width = acts.shape
    columns = grads.shape[1]
    blocks = NZH * NY
    span = width // (blocks * NC)
    rows = span // NX
    half = blocks // 2
    vmem = pl.BlockSpec(memory_space=pltpu.VMEM)
    moving = pl.BlockSpec((half, rows, columns), lambda j, where: (j, 0, 0))
    still = pl.BlockSpec((half, rows, columns), lambda j, where: (0, 0, 0))
    whole = jax.ShapeDtypeStruct((blocks, rows, columns), jnp.bfloat16)
    part = jax.ShapeDtypeStruct((half, rows, columns), jnp.bfloat16)
    return pl.pallas_call(
        functools.partial(partial_kernel, factor),
        out_shape=[whole, whole, whole, part, part],
        grid_spec=pltpu.PrefetchScalarGridSpec(
            num_scalar_prefetch=1,
            grid=(2,),
            in_specs=[vmem] * 4,
            out_specs=[moving, moving, moving, still, still],
            scratch_shapes=[
                pltpu.VMEM((2 * tokens, half * span), jnp.bfloat16),
                pltpu.VMEM((2 * tokens, columns), jnp.bfloat16),
            ],
        ),
        compiler_params=pltpu.CompilerParams(vmem_limit_bytes=VMEM_LIMIT),
        cost_estimate=pl.CostEstimate(
            flops=4 * tokens * columns * span * blocks,
            bytes_accessed=2 * blocks * span * columns + 4 * tokens * width,
            transcendentals=0,
        ),
        name="partials",
    )(where, acts, acts_in, grads, grads_in)


def sum_kernel(own, right, left, *outs):
    total = own[...].astype(jnp.float32) + right[...].astype(jnp.float32)
    total = (total + left[...].astype(jnp.float32)).astype(own.dtype)
    for k, out in enumerate(outs):

        @pl.when(pl.program_id(0) == k)
        def _():
            out[...] = total


def sums(own, right, left):
    blocks, rows, columns = own.shape
    each = blocks // NY
    moving = pl.BlockSpec((each, rows, columns), lambda k: (k, 0, 0))
    still = pl.BlockSpec((each, rows, columns), lambda k: (0, 0, 0))
    return pl.pallas_call(
        sum_kernel,
        out_shape=[jax.ShapeDtypeStruct((each, rows, columns), own.dtype)] * NY,
        grid=(NY,),
        in_specs=[moving] * 3,
        out_specs=[still] * NY,
        compiler_params=pltpu.CompilerParams(vmem_limit_bytes=VMEM_LIMIT),
        cost_estimate=pl.CostEstimate(
            flops=2 * 10**10, bytes_accessed=8 * blocks * rows * columns, transcendentals=0
        ),
        name="sums",
    )(own, right, left)


def input_kernel(where, grads, weight, *rest):
    out = rest[-1]
    pieces, groups, rows, columns = weight.shape
    span = pieces * rows
    for group in range(groups):
        block = weight[:, group].reshape(span, columns)
        out[:, group * span : (group + 1) * span] = lax.dot_general(
            grads[...], block, (((1,), (1,)), ((), ())), preferred_element_type=jnp.float32
        ).astype(out.dtype)


def input_half(where, grads, weight, width, before=None):
    tokens, columns = grads.shape
    pieces, groups, rows, _ = weight.shape
    steps = 4
    each = groups // steps
    block = each * pieces * rows
    in_specs = [
        pl.BlockSpec((tokens, columns), lambda j, where: (0, 0)),
        pl.BlockSpec((pieces, each, rows, columns), lambda j, where: (0, j, 0, 0)),
    ]
    args = [where, grads, weight]
    aliases = {}
    if before is not None:
        in_specs.append(pl.BlockSpec(memory_space=pl.ANY))
        args.append(before)
        aliases = {3: 0}
    return pl.pallas_call(
        input_kernel,
        out_shape=jax.ShapeDtypeStruct((tokens, width), jnp.bfloat16),
        grid_spec=pltpu.PrefetchScalarGridSpec(
            num_scalar_prefetch=1,
            grid=(steps,),
            in_specs=in_specs,
            out_specs=pl.BlockSpec((tokens, block), lambda j, where: (0, where[0] * steps + j)),
        ),
        input_output_aliases=aliases,
        compiler_params=pltpu.CompilerParams(vmem_limit_bytes=VMEM_LIMIT),
        cost_estimate=pl.CostEstimate(
            flops=2 * tokens * columns * pieces * groups * rows,
            bytes_accessed=2 * pieces * groups * rows * columns + 4 * tokens * columns,
            transcendentals=0,
        ),
        name="input_half",
    )(*args)


def shards(acts, grads_out, quant, scales):
    tokens, width = acts.shape
    columns = grads_out.shape[1]
    shard_rows = quant.shape[0]
    total_tokens = tokens * lax.axis_size(AXES)
    x, zh, y, c = (lax.axis_index(name) for name in ("x", "zh", "y", "c"))
    bf16 = jnp.bfloat16
    where = jnp.stack([c, x, y]).astype(jnp.int32)
    groups = NY * NC

    acts_in = shift(acts, "c", 1)
    grads_in = shift(grads_out, "c", 1)
    weight, quarter = weights(where, quant, scales)
    own_half = lax.all_gather(weight, ("y", "c"), axis=0, tiled=True)

    own, right, left, far_a, far_b = partials(
        where, acts, acts_in, grads_out, grads_in, 1.0 / math.sqrt(total_tokens)
    )
    near_a, near_b = shift(far_a, "x", 1), shift(far_b, "x", -1)
    quarter = chip_shift(quarter, lambda i, z: (i, (z + NZL) % NZ))
    half = far_a.shape[0]
    right = jnp.concatenate([total_of([right[:half], near_a]).astype(bf16), right[half:]], axis=0)
    left = jnp.concatenate([left[:half], total_of([left[half:], near_b]).astype(bf16)], axis=0)
    grads_later, right, left = lax.optimization_barrier((grads_out, right, left))
    right, left = shift(right, "x", 1), shift(left, "x", -1)

    own_half = own_half.reshape(1, groups, shard_rows, columns)
    grad_input = input_half(zh[None].astype(jnp.int32), grads_later, own_half, width)
    quarter, grad_input = lax.optimization_barrier((quarter, grad_input))
    grad_input, right, left = lax.optimization_barrier((grad_input, right, left))
    other_half = lax.all_gather(quarter, ("x", "y", "c"), axis=0, tiled=True)

    summed = sums(own, right, left)
    received = [summed[0]] + [shift(summed[k], "y", k) for k in (1, 3, 2)]
    rows = total_of(received).astype(bf16).reshape(NZH, NZL, 8, columns)
    rows = lax.all_to_all(rows.swapaxes(0, 1), "zl", split_axis=0, concat_axis=0, tiled=True)
    rows = jnp.sum(rows, axis=0, dtype=jnp.float32)
    away = chip_shift(pick(rows, 1 - zh, 0), lambda i, z: (i, (z + NZL) % NZ))
    other_half = other_half.reshape(NX, groups, shard_rows // NX, columns)
    grad_input = input_half(
        (1 - zh)[None].astype(jnp.int32), grads_later, other_half, width, grad_input
    )
    grad_input, away = lax.optimization_barrier((grad_input, away))
    weight_grad = pick(rows, zh, 0) + away
    return (grad_input, weight_grad)


def solution(mesh):
    fine = Mesh(mesh.devices.reshape(NX, NZL, NZH, NY, NC), AXES)
    tokens = P(AXES, None)
    rows = P(("zh", "y", "c"), None)
    return jax.shard_map(
        shards,
        mesh=fine,
        in_specs=(tokens, tokens, rows, rows),
        out_specs=(tokens, P(("zh", "y", "c", "x", "zl"), None)),
        check_vma=False,
    )
```

```python
import functools
import math

import jax
import jax.numpy as jnp
from jax import lax
from jax.experimental import pallas as pl
from jax.experimental.pallas import tpu as pltpu
from jax.sharding import Mesh
from jax.sharding import PartitionSpec as P

BLOCK = 128
NX, NZL, NZH, NY, NC = 4, 8, 2, 4, 2
NZ = NZL * NZH
AXES = ("x", "zl", "zh", "y", "c")
MIB = 1024 * 1024


def shift(value, axis, step):
    size = lax.axis_size(axis)
    return lax.ppermute(value, axis, [(i, (i + step) % size) for i in range(size)])


def chip_shift(value, move):
    def index(x, z, y, c):
        return (((x * NZL + z % NZL) * NZH + z // NZL) * NY + y) * NC + c

    pairs = []
    for x in range(NX):
        for z in range(NZ):
            to_x, to_z = move(x, z)
            for y in range(NY):
                for c in range(NC):
                    pairs.append((index(x, z, y, c), index(to_x, to_z, y, c)))
    return lax.ppermute(value, AXES, pairs)


def weight_kernel(where, quant, scales, weight, quarter):
    rows, columns = quant.shape
    levels = quant[...].astype(jnp.float32)
    factors = scales[...].T
    for block in range(columns // BLOCK):
        run = slice(block * BLOCK, (block + 1) * BLOCK)
        weight[:, run] = (levels[:, run] * factors[:, block : block + 1]).astype(weight.dtype)
    part = quarter.shape[0]
    quarter[...] = weight[pl.ds(pl.multiple_of(where[1] * part, part), part), :]


def weights(where, quant, scales):
    rows, columns = quant.shape
    vmem = pl.BlockSpec(memory_space=pltpu.VMEM)
    return pl.pallas_call(
        weight_kernel,
        out_shape=[
            jax.ShapeDtypeStruct((rows, columns), jnp.bfloat16),
            jax.ShapeDtypeStruct((rows // NX, columns), jnp.bfloat16),
        ],
        in_specs=[pl.BlockSpec(memory_space=pltpu.SMEM), vmem, vmem],
        out_specs=[vmem, vmem],
        compiler_params=pltpu.CompilerParams(vmem_limit_bytes=58 * MIB),
        cost_estimate=pl.CostEstimate(
            flops=rows * columns, bytes_accessed=4 * rows * columns, transcendentals=0
        ),
        name="weights",
    )(where, quant, scales.T)


def partial_kernel(factor, where, acts, acts_in, grads, grads_in, out, lhs, rhs):
    step = pl.program_id(0)
    tokens = acts.shape[0]
    _, blocks, rows, _ = out.shape
    span = rows * NX

    @pl.when(step == 0)
    def _():
        rhs[:tokens] = grads[...]
        rhs[tokens:] = grads_in[...]

    for t in range(blocks):
        j = step * blocks + t
        block = (j % NZH) * NY + j // NZH
        start = pl.multiple_of((block * NC + where[0]) * span, span)
        lhs[:tokens, t * span : (t + 1) * span] = acts[:, pl.ds(start, span)]
        lhs[tokens:, t * span : (t + 1) * span] = acts_in[:, pl.ds(start, span)]
    value = lax.dot_general(
        lhs[...], rhs[...], (((0,), (0,)), ((), ())), preferred_element_type=jnp.float32
    )
    value = (value * factor).astype(out.dtype)
    for t in range(blocks):
        for x in range(NX):
            start = t * span + x * rows
            out[x, t] = value[start : start + rows]


def partials(where, acts, acts_in, grads, grads_in, factor):
    tokens, width = acts.shape
    columns = grads.shape[1]
    blocks = NZH * NY
    span = width // (blocks * NC)
    rows = span // NX
    half = blocks // 2
    vmem = pl.BlockSpec(memory_space=pltpu.VMEM)
    return pl.pallas_call(
        functools.partial(partial_kernel, factor),
        out_shape=jax.ShapeDtypeStruct((NX, blocks, rows, columns), jnp.bfloat16),
        grid_spec=pltpu.PrefetchScalarGridSpec(
            num_scalar_prefetch=1,
            grid=(2,),
            in_specs=[vmem] * 4,
            out_specs=pl.BlockSpec((NX, half, rows, columns), lambda j, where: (0, j, 0, 0)),
            scratch_shapes=[
                pltpu.VMEM((2 * tokens, half * span), jnp.bfloat16),
                pltpu.VMEM((2 * tokens, columns), jnp.bfloat16),
            ],
        ),
        compiler_params=pltpu.CompilerParams(vmem_limit_bytes=58 * MIB),
        cost_estimate=pl.CostEstimate(
            flops=4 * tokens * columns * span * blocks,
            bytes_accessed=2 * blocks * span * columns + 4 * tokens * width,
            transcendentals=0,
        ),
        name="partials",
    )(where, acts, acts_in, grads, grads_in)


def sum_kernel(parts, out):
    total = parts[0].astype(jnp.float32)
    for k in range(1, parts.shape[0]):
        total = total + parts[k].astype(jnp.float32)
    out[...] = total.astype(out.dtype)


def sums(parts):
    count, rows, columns = parts.shape
    each = min(rows, 128)
    return pl.pallas_call(
        sum_kernel,
        out_shape=jax.ShapeDtypeStruct((rows, columns), parts.dtype),
        grid=(rows // each,),
        in_specs=[pl.BlockSpec((count, each, columns), lambda k: (0, k, 0))],
        out_specs=pl.BlockSpec((each, columns), lambda k: (k, 0)),
        compiler_params=pltpu.CompilerParams(vmem_limit_bytes=16 * MIB),
        cost_estimate=pl.CostEstimate(
            flops=2 * 10**10, bytes_accessed=2 * count * rows * columns, transcendentals=0
        ),
        name="sums",
    )(parts)


def input_kernel(where, grads, weight, *rest):
    out = rest[-1]
    pieces, groups, rows, columns = weight.shape
    span = pieces * rows
    for group in range(groups):
        block = weight[:, group].reshape(span, columns)
        out[:, group * span : (group + 1) * span] = lax.dot_general(
            grads[...], block, (((1,), (1,)), ((), ())), preferred_element_type=jnp.float32
        ).astype(out.dtype)


def input_half(where, grads, weight, width, before=None):
    tokens, columns = grads.shape
    pieces, groups, rows, _ = weight.shape
    steps = 4
    each = groups // steps
    block = each * pieces * rows
    in_specs = [
        pl.BlockSpec((tokens, columns), lambda j, where: (0, 0)),
        pl.BlockSpec((pieces, each, rows, columns), lambda j, where: (0, j, 0, 0)),
    ]
    args = [where, grads, weight]
    aliases = {}
    if before is not None:
        in_specs.append(pl.BlockSpec(memory_space=pl.ANY))
        args.append(before)
        aliases = {3: 0}
    return pl.pallas_call(
        input_kernel,
        out_shape=jax.ShapeDtypeStruct((tokens, width), jnp.bfloat16),
        grid_spec=pltpu.PrefetchScalarGridSpec(
            num_scalar_prefetch=1,
            grid=(steps,),
            in_specs=in_specs,
            out_specs=pl.BlockSpec((tokens, block), lambda j, where: (0, where[0] * steps + j)),
        ),
        input_output_aliases=aliases,
        compiler_params=pltpu.CompilerParams(vmem_limit_bytes=58 * MIB),
        cost_estimate=pl.CostEstimate(
            flops=2 * tokens * columns * pieces * groups * rows,
            bytes_accessed=2 * pieces * groups * rows * columns + 4 * tokens * columns,
            transcendentals=0,
        ),
        name="input_half",
    )(*args)


def shards(acts, grads_out, quant, scales):
    tokens, width = acts.shape
    columns = grads_out.shape[1]
    shard_rows = quant.shape[0]
    total_tokens = tokens * lax.axis_size(AXES)
    x, zh, c = (lax.axis_index(name) for name in ("x", "zh", "c"))
    where = jnp.stack([c, x]).astype(jnp.int32)
    groups = NY * NC

    acts_in = shift(acts, "c", 1)
    grads_in = shift(grads_out, "c", 1)
    weight, quarter = weights(where, quant, scales)
    own_half = lax.all_gather(weight, ("y", "c"), axis=0, tiled=True)

    parts = partials(where, acts, acts_in, grads_out, grads_in, 1.0 / math.sqrt(total_tokens))
    received = lax.all_to_all(parts, "x", split_axis=0, concat_axis=0, tiled=True)
    quarter = chip_shift(quarter, lambda i, z: (i, (z + NZL) % NZ))
    other_half = lax.all_gather(quarter, ("x", "y", "c"), axis=0, tiled=True)
    own_half = own_half.reshape(1, groups, shard_rows, columns)
    grad_input = input_half(zh[None].astype(jnp.int32), grads_out, own_half, width)
    grad_input, received = lax.optimization_barrier((grad_input, received))
    chunk = NZH * NZL * 8
    summed = sums(received.reshape(NX, NY * chunk, columns)).reshape(NY, chunk, columns)
    received = lax.all_to_all(summed, "y", split_axis=0, concat_axis=0, tiled=True)
    rows = sums(received).reshape(NZ, 8, columns)
    rows = lax.all_to_all(rows, ("zh", "zl"), split_axis=0, concat_axis=0, tiled=True)
    other_half = other_half.reshape(NX, groups, shard_rows // NX, columns)
    grad_input = input_half(
        (1 - zh)[None].astype(jnp.int32), grads_out, other_half, width, grad_input
    )
    grad_input, rows = lax.optimization_barrier((grad_input, rows))
    weight_grad = jnp.sum(rows, axis=0, dtype=jnp.float32)
    return (grad_input, weight_grad)


def solution(mesh):
    fine = Mesh(mesh.devices.reshape(NX, NZL, NZH, NY, NC), AXES)
    tokens = P(AXES, None)
    rows = P(("zh", "y", "c"), None)
    return jax.shard_map(
        shards,
        mesh=fine,
        in_specs=(tokens, tokens, rows, rows),
        out_specs=(tokens, P(("zh", "y", "c", "x", "zl"), None)),
        check_vma=False,
    )
```

```python
import functools
import math

import jax
import jax.numpy as jnp
from jax import lax
from jax.experimental import pallas as pl
from jax.experimental.pallas import tpu as pltpu
from jax.sharding import Mesh
from jax.sharding import PartitionSpec as P

BLOCK = 128
NX, NZL, NZH, NY, NC = 4, 8, 2, 4, 2
NZ = NZL * NZH
AXES = ("x", "zl", "zh", "y", "c")
MIB = 1024 * 1024


def shift(value, axis, step):
    size = lax.axis_size(axis)
    return lax.ppermute(value, axis, [(i, (i + step) % size) for i in range(size)])


def chip_shift(value, move):
    def index(x, z, y, c):
        return (((x * NZL + z % NZL) * NZH + z // NZL) * NY + y) * NC + c

    pairs = []
    for x in range(NX):
        for z in range(NZ):
            to_x, to_z = move(x, z)
            for y in range(NY):
                for c in range(NC):
                    pairs.append((index(x, z, y, c), index(to_x, to_z, y, c)))
    return lax.ppermute(value, AXES, pairs)


def weight_kernel(odd, quant, scales, weight, half):
    rows, columns = quant.shape
    levels = quant[...].astype(jnp.float32)
    factors = scales[...].T
    for block in range(columns // BLOCK):
        run = slice(block * BLOCK, (block + 1) * BLOCK)
        weight[:, run] = (levels[:, run] * factors[:, block : block + 1]).astype(weight.dtype)
    part = half.shape[0]
    half[...] = weight[pl.ds(pl.multiple_of(odd[0] * part, part), part), :]


def weights(odd, quant, scales):
    rows, columns = quant.shape
    vmem = pl.BlockSpec(memory_space=pltpu.VMEM)
    quant, scales = (
        pltpu.with_memory_space_constraint(v, pltpu.HBM) for v in (quant, scales.T)
    )
    return pl.pallas_call(
        weight_kernel,
        out_shape=[
            jax.ShapeDtypeStruct((rows, columns), jnp.bfloat16),
            jax.ShapeDtypeStruct((rows // 2, columns), jnp.bfloat16),
        ],
        in_specs=[pl.BlockSpec(memory_space=pltpu.SMEM), vmem, vmem],
        out_specs=[vmem, vmem],
        compiler_params=pltpu.CompilerParams(vmem_limit_bytes=8 * MIB),
        cost_estimate=pl.CostEstimate(
            flops=rows * columns, bytes_accessed=4 * rows * columns, transcendentals=0
        ),
        name="weights",
    )(odd, quant, scales)


def partial_kernel(factor, core, acts, acts_in, grads, grads_in, out, lhs, rhs, sems):
    step = pl.program_id(0)
    tokens = acts.shape[0]
    _, blocks, rows, _ = out.shape
    span = rows * NX

    def copies(at):
        found = []
        for t in range(blocks):
            j = at * blocks + t
            block = (j % NZH) * NY + j // NZH
            start = pl.multiple_of((block * NC + core[0]) * span, span)
            for half, source in enumerate((acts, acts_in)):
                found.append(
                    pltpu.make_async_copy(
                        source.at[:, pl.ds(start, span)],
                        lhs.at[at, pl.ds(half * tokens, tokens), pl.ds(t * span, span)],
                        sems.at[2 * j + half],
                    )
                )
        return found

    base = 4 * blocks
    right = [
        pltpu.make_async_copy(
            source, rhs.at[pl.ds(half * tokens, tokens)], sems.at[base + half]
        )
        for half, source in enumerate((grads, grads_in))
    ]

    @pl.when(step == 0)
    def _():
        for copy in right + copies(0) + copies(1):
            copy.start()
        for copy in right + copies(0):
            copy.wait()

    @pl.when(step == 1)
    def _():
        for copy in copies(1):
            copy.wait()

    value = lax.dot_general(
        lhs[step], rhs[...], (((0,), (0,)), ((), ())), preferred_element_type=jnp.float32
    )
    value = (value * factor).astype(out.dtype)
    for t in range(blocks):
        for x in range(NX):
            start = t * span + x * rows
            out[x, t] = value[start : start + rows]


def partials(core, acts, acts_in, grads, grads_in, factor):
    tokens, width = acts.shape
    columns = grads.shape[1]
    blocks = NZH * NY
    span = width // (blocks * NC)
    rows = span // NX
    half = blocks // 2
    acts, grads = (pltpu.with_memory_space_constraint(v, pltpu.HBM) for v in (acts, grads))
    return pl.pallas_call(
        functools.partial(partial_kernel, factor),
        out_shape=pltpu.HBM((NX, blocks, rows, columns), jnp.bfloat16),
        grid_spec=pltpu.PrefetchScalarGridSpec(
            num_scalar_prefetch=1,
            grid=(2,),
            in_specs=[pl.BlockSpec(memory_space=pl.ANY)] * 4,
            out_specs=pl.BlockSpec((NX, half, rows, columns), lambda j, core: (0, j, 0, 0)),
            scratch_shapes=[
                pltpu.VMEM((2, 2 * tokens, half * span), jnp.bfloat16),
                pltpu.VMEM((2 * tokens, columns), jnp.bfloat16),
                pltpu.SemaphoreType.DMA((2 * blocks + 2,)),
            ],
        ),
        compiler_params=pltpu.CompilerParams(vmem_limit_bytes=24 * MIB),
        cost_estimate=pl.CostEstimate(
            flops=4 * tokens * columns * span * blocks,
            bytes_accessed=2 * blocks * span * columns + 4 * tokens * width,
            transcendentals=0,
        ),
        name="partials",
    )(core, acts, acts_in, grads, grads_in)


def sum_kernel(parts, out, held, sems):
    count = parts.shape[0]
    pieces, _, rows, _ = held.shape
    copies = [
        pltpu.make_async_copy(parts.at[:, pl.ds(q * rows, rows)], held.at[q], sems.at[q])
        for q in range(pieces)
    ]
    for copy in copies:
        copy.start()
    for q, copy in enumerate(copies):
        copy.wait()
        total = held[q, 0].astype(jnp.float32)
        for k in range(1, count):
            total = total + held[q, k].astype(jnp.float32)
        out[q * rows : (q + 1) * rows] = total.astype(out.dtype)


def sums(parts):
    count, rows, columns = parts.shape
    each = min(rows, 64)
    pieces = rows // each
    return pl.pallas_call(
        sum_kernel,
        out_shape=jax.ShapeDtypeStruct((rows, columns), parts.dtype),
        in_specs=[pl.BlockSpec(memory_space=pl.ANY)],
        out_specs=pl.BlockSpec(memory_space=pltpu.VMEM),
        scratch_shapes=[
            pltpu.VMEM((pieces, count, each, columns), parts.dtype),
            pltpu.SemaphoreType.DMA((pieces,)),
        ],
        compiler_params=pltpu.CompilerParams(vmem_limit_bytes=16 * MIB),
        cost_estimate=pl.CostEstimate(
            flops=2 * 10**10, bytes_accessed=2 * count * rows * columns, transcendentals=0
        ),
        name="sums",
    )(parts)


def input_kernel(where, grads, weight, *rest):
    out, held, lhs, result, in_sems, out_sems = rest[-6:]
    groups, pieces, rows, _ = weight.shape
    span = pieces * rows
    width = groups * span
    first = pltpu.make_async_copy(grads, lhs, in_sems.at[groups])
    first.start()
    copies = [
        pltpu.make_async_copy(weight.at[group], held.at[group], in_sems.at[group])
        for group in range(groups)
    ]
    for copy in copies:
        copy.start()
    first.wait()
    done = []
    for group, copy in enumerate(copies):
        copy.wait()
        for piece in range(pieces):
            start = group * span + piece * rows
            block = held[group, lax.rem(piece + where[1], pieces)]
            result[:, start : start + rows] = lax.dot_general(
                lhs[...], block, (((1,), (1,)), ((), ())), preferred_element_type=jnp.float32
            ).astype(result.dtype)
        start = pl.multiple_of(where[0] * width + group * span, span)
        done.append(
            pltpu.make_async_copy(
                result.at[:, pl.ds(group * span, span)],
                out.at[:, pl.ds(start, span)],
                out_sems.at[group],
            )
        )
        done[-1].start()
    for copy in done:
        copy.wait()


def input_half(where, grads, weight, width, before=None):
    tokens, columns = grads.shape
    groups, pieces, rows, _ = weight.shape
    weight = pltpu.with_memory_space_constraint(weight, pltpu.HBM)
    args = [where, grads, weight]
    aliases = {}
    if before is not None:
        args.append(before)
        aliases = {3: 0}
    anywhere = pl.BlockSpec(memory_space=pl.ANY)
    return pl.pallas_call(
        input_kernel,
        out_shape=jax.ShapeDtypeStruct((tokens, width), jnp.bfloat16),
        in_specs=[pl.BlockSpec(memory_space=pltpu.SMEM)] + [anywhere] * (len(args) - 1),
        out_specs=anywhere,
        scratch_shapes=[
            pltpu.VMEM((groups, pieces, rows, columns), jnp.bfloat16),
            pltpu.VMEM((tokens, columns), jnp.bfloat16),
            pltpu.VMEM((tokens, groups * pieces * rows), jnp.bfloat16),
            pltpu.SemaphoreType.DMA((groups + 1,)),
            pltpu.SemaphoreType.DMA((groups,)),
        ],
        input_output_aliases=aliases,
        compiler_params=pltpu.CompilerParams(vmem_limit_bytes=16 * MIB),
        cost_estimate=pl.CostEstimate(
            flops=2 * tokens * columns * pieces * groups * rows,
            bytes_accessed=2 * pieces * groups * rows * columns + 4 * tokens * columns,
            transcendentals=0,
        ),
        name="input_half",
    )(*args)


def shards(acts, grads_out, quant, scales):
    tokens, width = acts.shape
    columns = grads_out.shape[1]
    shard_rows = quant.shape[0]
    total_tokens = tokens * lax.axis_size(AXES)
    zl, zh, c = (lax.axis_index(name) for name in ("zl", "zh", "c"))
    odd = zl % 2
    groups = NY * NC

    acts_in = shift(acts, "c", 1)
    grads_in = shift(grads_out, "c", 1)
    weight, piece = weights(odd[None].astype(jnp.int32), quant, scales)
    own_half = lax.all_gather(weight, ("y", "c"), axis=0, tiled=True)
    factor = 1.0 / math.sqrt(total_tokens)
    parts = partials(c[None].astype(jnp.int32), acts, acts_in, grads_out, grads_in, factor)
    received = lax.all_to_all(parts, "x", split_axis=0, concat_axis=0, tiled=True)
    first = chip_shift(piece, lambda i, z: (i, (z + NZL) % NZ))
    second = chip_shift(first, lambda i, z: (i, z ^ 1))
    other_half = lax.all_gather(
        jnp.concatenate([first, second], axis=0), ("y", "c"), axis=0, tiled=True
    )
    chunk = NZH * NZL * 8
    summed = sums(received.reshape(NX, NY * chunk, columns)).reshape(NY, chunk, columns)
    grads_later, summed = lax.optimization_barrier((grads_out, summed))
    received = lax.all_to_all(summed, "y", split_axis=0, concat_axis=0, tiled=True)
    own_half = own_half.reshape(groups, 1, shard_rows, columns)
    place = jnp.stack([zh, 0 * odd]).astype(jnp.int32)
    grad_input = input_half(place, grads_later, own_half, width)
    grad_input, received = lax.optimization_barrier((grad_input, received))
    rows = sums(received).reshape(NZ, 8, columns)
    rows = lax.all_to_all(rows, ("zh", "zl"), split_axis=0, concat_axis=0, tiled=True)
    other_half = other_half.reshape(groups, 2, shard_rows // 2, columns)
    place = jnp.stack([1 - zh, odd]).astype(jnp.int32)
    grad_input = input_half(place, grads_later, other_half, width, grad_input)
    grad_input, rows = lax.optimization_barrier((grad_input, rows))
    weight_grad = jnp.sum(rows, axis=0, dtype=jnp.float32)
    return (grad_input, weight_grad)


def solution(mesh):
    fine = Mesh(mesh.devices.reshape(NX, NZL, NZH, NY, NC), AXES)
    tokens = P(AXES, None)
    rows = P(("zh", "y", "c"), None)
    return jax.shard_map(
        shards,
        mesh=fine,
        in_specs=(tokens, tokens, rows, rows),
        out_specs=(tokens, P(("zh", "y", "c", "x", "zl"), None)),
        check_vma=False,
    )
```

```python
import functools
import math

import jax
import jax.numpy as jnp
from jax import lax
from jax.experimental import pallas as pl
from jax.experimental.pallas import tpu as pltpu
from jax.sharding import Mesh
from jax.sharding import PartitionSpec as P

BLOCK = 128
NX, NZL, NZH, NY, NC = 4, 8, 2, 4, 2
NZ = NZL * NZH
AXES = ("x", "zl", "zh", "y", "c")
MIB = 1024 * 1024
AHEAD = 3
LEFT = 640
CHAIN = 3 * 10**10


def shift(value, axis, step):
    size = lax.axis_size(axis)
    return lax.ppermute(value, axis, [(i, (i + step) % size) for i in range(size)])


def chip_shift(value, move):
    def index(x, z, y, c):
        return (((x * NZL + z % NZL) * NZH + z // NZL) * NY + y) * NC + c

    pairs = []
    for x in range(NX):
        for z in range(NZ):
            to_x, to_z = move(x, z)
            for y in range(NY):
                for c in range(NC):
                    pairs.append((index(x, z, y, c), index(to_x, to_z, y, c)))
    return lax.ppermute(value, AXES, pairs)


def total_of(parts, dtype):
    total = parts[0].astype(jnp.float32)
    for part in parts[1:]:
        total = total + part.astype(jnp.float32)
    return total.astype(dtype)


def weight_kernel(odd, quant, scales, weight, half):
    rows, columns = quant.shape
    levels = quant[...].astype(jnp.float32)
    factors = scales[...].T
    for block in range(columns // BLOCK):
        run = slice(block * BLOCK, (block + 1) * BLOCK)
        weight[:, run] = (levels[:, run] * factors[:, block : block + 1]).astype(weight.dtype)
    part = half.shape[0]
    half[...] = weight[pl.ds(pl.multiple_of(odd[0] * part, part), part), :]


def weights(odd, quant, scales):
    rows, columns = quant.shape
    vmem = pl.BlockSpec(memory_space=pltpu.VMEM)
    quant, scales = (
        pltpu.with_memory_space_constraint(v, pltpu.HBM) for v in (quant, scales.T)
    )
    return pl.pallas_call(
        weight_kernel,
        out_shape=[
            jax.ShapeDtypeStruct((rows, columns), jnp.bfloat16),
            jax.ShapeDtypeStruct((rows // 2, columns), jnp.bfloat16),
        ],
        in_specs=[pl.BlockSpec(memory_space=pltpu.SMEM), vmem, vmem],
        out_specs=[vmem, vmem],
        compiler_params=pltpu.CompilerParams(vmem_limit_bytes=8 * MIB),
        cost_estimate=pl.CostEstimate(
            flops=rows * columns, bytes_accessed=4 * rows * columns, transcendentals=0
        ),
        name="weights",
    )(odd, quant, scales)


def partial_kernel(
    factor, where, acts, acts_in, grads, grads_in, left, r0, r1, r2, r3, *scratch
):
    lhs, rhs, lbuf, rbuf, in_sems, out_sems = scratch
    tokens = acts.shape[0]
    steps = lhs.shape[0]
    each = NY * NZH // steps
    _, _, rows, cut = left.shape
    span = rows * NX
    core, x, y = where[0], where[1], where[2]
    row_group = [lax.rem(k + NX - x, NX) for k in range(NX)]

    first = [
        pltpu.make_async_copy(
            source, rhs.at[pl.ds(half * tokens, tokens)], in_sems.at[2 * NY * NZH + half]
        )
        for half, source in enumerate((grads, grads_in))
    ]
    for copy in first:
        copy.start()
    loads = []
    for j in range(NY * NZH):
        block = j % NZH * NY + lax.rem(y + j // NZH, NY)
        start = pl.multiple_of((block * NC + core) * span, span)
        for half, source in enumerate((acts, acts_in)):
            loads.append(
                pltpu.make_async_copy(
                    source.at[:, pl.ds(start, span)],
                    lhs.at[j // each, pl.ds(half * tokens, tokens), pl.ds(j % each * span, span)],
                    in_sems.at[2 * j + half],
                )
            )
            loads[-1].start()
    for copy in first:
        copy.wait()
    stores = []
    for step in range(steps):
        for copy in loads[2 * each * step : 2 * each * (step + 1)]:
            copy.wait()
        value = lax.dot_general(
            lhs[step], rhs[...], (((0,), (0,)), ((), ())), preferred_element_type=jnp.float32
        )
        value = (value * factor).astype(left.dtype)
        for t in range(each):
            j = step * each + t
            k, z_hi = j // NZH, j % NZH
            for group in range(NX):
                start = t * span + group * rows
                lbuf[j, group] = value[start : start + rows, :cut]
                rbuf[k, row_group[group] * NZH + z_hi] = value[start : start + rows, cut:]
            place = lax.rem(y + k, NY) * NZH + z_hi
            stores.append(
                pltpu.make_async_copy(lbuf.at[j], left.at[:, place], out_sems.at[NY + j])
            )
            stores[-1].start()
            if z_hi == NZH - 1:
                stores.append(
                    pltpu.make_async_copy(rbuf.at[k], (r0, r1, r2, r3)[k], out_sems.at[k])
                )
                stores[-1].start()
    for copy in stores:
        copy.wait()


def partials(where, acts, acts_in, grads, grads_in, factor):
    tokens, width = acts.shape
    columns = grads.shape[1]
    blocks = NZH * NY
    span = width // (blocks * NC)
    rows = span // NX
    steps = 2
    cut = LEFT
    acts, grads = (pltpu.with_memory_space_constraint(v, pltpu.HBM) for v in (acts, grads))
    anywhere = pl.BlockSpec(memory_space=pl.ANY)
    right = (NX * NZH, rows, columns - cut)
    return pl.pallas_call(
        functools.partial(partial_kernel, factor),
        out_shape=[pltpu.HBM((NX, blocks, rows, cut), jnp.bfloat16)]
        + [pltpu.HBM(right, jnp.bfloat16)] * NY,
        in_specs=[pl.BlockSpec(memory_space=pltpu.SMEM)] + [anywhere] * 4,
        out_specs=[anywhere] * (1 + NY),
        scratch_shapes=[
            pltpu.VMEM((steps, 2 * tokens, blocks // steps * span), jnp.bfloat16),
            pltpu.VMEM((2 * tokens, columns), jnp.bfloat16),
            pltpu.VMEM((blocks, NX, rows, cut), jnp.bfloat16),
            pltpu.VMEM((NY, *right), jnp.bfloat16),
            pltpu.SemaphoreType.DMA((2 * blocks + 2,)),
            pltpu.SemaphoreType.DMA((blocks + NY,)),
        ],
        compiler_params=pltpu.CompilerParams(vmem_limit_bytes=24 * MIB),
        cost_estimate=pl.CostEstimate(
            flops=4 * tokens * columns * span * blocks,
            bytes_accessed=2 * blocks * span * columns + 4 * tokens * width,
            transcendentals=0,
        ),
        name="partials",
    )(where, acts, acts_in, grads, grads_in)


def left_kernel(parts, out, held, sems):
    pieces, terms, rows, columns = held.shape
    copies = [
        pltpu.make_async_copy(parts.at[:, pl.ds(q * rows, rows)], held.at[q], sems.at[q])
        for q in range(pieces)
    ]
    for copy in copies[:AHEAD]:
        copy.start()
    for q, copy in enumerate(copies):
        if q + AHEAD < pieces:
            copies[q + AHEAD].start()
        copy.wait()
        out[q * rows : (q + 1) * rows] = total_of([held[q, k] for k in range(terms)], out.dtype)


def left_sums(parts):
    terms, rows, columns = parts.shape
    pieces = 4
    return pl.pallas_call(
        left_kernel,
        out_shape=jax.ShapeDtypeStruct((rows, columns), parts.dtype),
        in_specs=[pl.BlockSpec(memory_space=pl.ANY)],
        out_specs=pl.BlockSpec(memory_space=pltpu.VMEM),
        scratch_shapes=[
            pltpu.VMEM((pieces, terms, rows // pieces, columns), parts.dtype),
            pltpu.SemaphoreType.DMA((pieces,)),
        ],
        compiler_params=pltpu.CompilerParams(vmem_limit_bytes=16 * MIB),
        cost_estimate=pl.CostEstimate(
            flops=CHAIN, bytes_accessed=2 * terms * rows * columns, transcendentals=0
        ),
        name="left_sums",
    )(parts)


def right_kernel(*refs):
    count = len(refs) // 2
    parts, outs = refs[:count], refs[count:]
    rows = outs[0].shape[0]
    for k, out in enumerate(outs):
        run = slice(k * rows, (k + 1) * rows)
        out[...] = total_of([part[run] for part in parts], out.dtype)


def right_sums(parts):
    rows, columns = parts[0].shape
    vmem = pl.BlockSpec(memory_space=pltpu.VMEM)
    count = len(parts)
    return pl.pallas_call(
        right_kernel,
        out_shape=[jax.ShapeDtypeStruct((rows // count, columns), parts[0].dtype)] * count,
        in_specs=[vmem] * count,
        out_specs=[vmem] * count,
        compiler_params=pltpu.CompilerParams(vmem_limit_bytes=16 * MIB),
        cost_estimate=pl.CostEstimate(
            flops=CHAIN, bytes_accessed=2 * count * rows * columns, transcendentals=0
        ),
        name="right_sums",
    )(*parts)


def joined_kernel(left, *refs):
    parts, out = refs[:-1], refs[-1]
    cut = left.shape[2]
    out[:, :cut] = total_of([left[k] for k in range(left.shape[0])], out.dtype)
    out[:, cut:] = total_of([part[...] for part in parts], out.dtype)


def joined_sums(left, parts):
    _, rows, cut = left.shape
    vmem = pl.BlockSpec(memory_space=pltpu.VMEM)
    return pl.pallas_call(
        joined_kernel,
        out_shape=jax.ShapeDtypeStruct((rows, cut + parts[0].shape[1]), left.dtype),
        in_specs=[vmem] * (1 + len(parts)),
        out_specs=vmem,
        compiler_params=pltpu.CompilerParams(vmem_limit_bytes=16 * MIB),
        cost_estimate=pl.CostEstimate(
            flops=CHAIN, bytes_accessed=10 * rows * 1024, transcendentals=0
        ),
        name="joined_sums",
    )(left, *parts)


def input_kernel(where, grads, weight, *rest):
    out, held, lhs, result, in_sems, out_sems = rest[-6:]
    units, each, rows, columns = held.shape
    pitch = out.shape[1] // (NZH * units * each)
    first = pltpu.make_async_copy(grads, lhs, in_sems.at[units])
    first.start()
    copies = [
        pltpu.make_async_copy(weight.at[unit], held.at[unit], in_sems.at[unit])
        for unit in range(units)
    ]
    for copy in copies[:AHEAD]:
        copy.start()
    first.wait()
    done = []
    for unit, copy in enumerate(copies):
        if unit + AHEAD < units:
            copies[unit + AHEAD].start()
        copy.wait()
        span = each * rows
        result[:, unit * span : (unit + 1) * span] = lax.dot_general(
            lhs[...],
            held[unit].reshape(span, columns),
            (((1,), (1,)), ((), ())),
            preferred_element_type=jnp.float32,
        ).astype(result.dtype)
        for group in range(unit * each, (unit + 1) * each):
            start = pl.multiple_of(where[0] * rows, rows) + group * pitch
            done.append(
                pltpu.make_async_copy(
                    result.at[:, pl.ds(group * rows, rows)],
                    out.at[:, pl.ds(pl.multiple_of(start, rows), rows)],
                    out_sems.at[group],
                )
            )
            done[-1].start()
    for copy in done:
        copy.wait()


def input_part(place, grads, weight, width, before=None):
    tokens, columns = grads.shape
    groups, rows, _ = weight.shape
    each = max(1, 256 // rows)
    units = groups // each
    weight = weight.reshape(units, each, rows, columns)
    weight = pltpu.with_memory_space_constraint(weight, pltpu.HBM)
    args = [place[None].astype(jnp.int32), grads, weight]
    aliases = {}
    if before is not None:
        args.append(before)
        aliases = {3: 0}
    anywhere = pl.BlockSpec(memory_space=pl.ANY)
    return pl.pallas_call(
        input_kernel,
        out_shape=jax.ShapeDtypeStruct((tokens, width), jnp.bfloat16),
        in_specs=[pl.BlockSpec(memory_space=pltpu.SMEM)] + [anywhere] * (len(args) - 1),
        out_specs=anywhere,
        scratch_shapes=[
            pltpu.VMEM((units, each, rows, columns), jnp.bfloat16),
            pltpu.VMEM((tokens, columns), jnp.bfloat16),
            pltpu.VMEM((tokens, groups * rows), jnp.bfloat16),
            pltpu.SemaphoreType.DMA((units + 1,)),
            pltpu.SemaphoreType.DMA((groups,)),
        ],
        input_output_aliases=aliases,
        compiler_params=pltpu.CompilerParams(vmem_limit_bytes=16 * MIB),
        cost_estimate=pl.CostEstimate(
            flops=2 * tokens * columns * groups * rows,
            bytes_accessed=2 * groups * rows * columns + 4 * tokens * columns,
            transcendentals=0,
        ),
        name="input_part",
    )(*args)


def shards(acts, grads_out, quant, scales):
    tokens, width = acts.shape
    columns = grads_out.shape[1]
    shard_rows = quant.shape[0]
    total_tokens = tokens * lax.axis_size(AXES)
    x, zl, zh, y, c = (lax.axis_index(name) for name in AXES)
    odd = zl % 2
    groups = NY * NC
    chunk = NZH * NZL * 8

    acts_in = shift(acts, "c", 1)
    grads_in = shift(grads_out, "c", 1)
    weight, piece = weights(odd[None].astype(jnp.int32), quant, scales)
    own_half = lax.all_gather(weight, ("y", "c"), axis=0, tiled=True)
    fetched = chip_shift(piece, lambda i, z: (i, (z + NZL) % NZ))

    factor = 1.0 / math.sqrt(total_tokens)
    where = jnp.stack([c, x, y]).astype(jnp.int32)
    where, _ = lax.optimization_barrier((where, weight))
    left, *right = partials(where, acts, acts_in, grads_out, grads_in, factor)
    left = lax.all_to_all(left, "x", split_axis=0, concat_axis=0, tiled=True)
    right = [right[0]] + [shift(right[k], "y", k) for k in (1, 3, 2)]

    fetched, _ = lax.optimization_barrier((fetched, right[1]))
    fetched_all = lax.all_gather(fetched, ("y", "c"), axis=0, tiled=True)
    fetched, *_ = lax.optimization_barrier((fetched, left, *right))
    swapped = chip_shift(fetched, lambda i, z: (i, z ^ 1))
    swapped_all = lax.all_gather(swapped, ("y", "c"), axis=0, tiled=True)

    left = left_sums(left.reshape(NX, NY * chunk, LEFT)).reshape(NY, chunk, LEFT)
    right = right_sums([part.reshape(NX * chunk, columns - LEFT) for part in right])
    grads_later, _ = lax.optimization_barrier((grads_out, left))
    left = lax.all_to_all(left, "y", split_axis=0, concat_axis=0, tiled=True)
    right = [right[0]] + [shift(right[k], "x", k) for k in (1, 3, 2)]
    own_half = own_half.reshape(groups, shard_rows, columns)
    grad_input = input_part(zh * groups, grads_later, own_half, width)
    grad_input, left = lax.optimization_barrier((grad_input, left))
    rows = joined_sums(left, right).reshape(NZ, 8, columns)
    rows = lax.all_to_all(rows, ("zh", "zl"), split_axis=0, concat_axis=0, tiled=True)
    base = 2 * groups * (1 - zh)
    for gathered, place in ((fetched_all, base + odd), (swapped_all, base + 1 - odd)):
        gathered = gathered.reshape(groups, shard_rows // 2, columns)
        grad_input = input_part(place, grads_later, gathered, width, grad_input)
    grad_input, rows = lax.optimization_barrier((grad_input, rows))
    weight_grad = jnp.sum(rows, axis=0, dtype=jnp.float32)
    return (grad_input, weight_grad)


def solution(mesh):
    fine = Mesh(mesh.devices.reshape(NX, NZL, NZH, NY, NC), AXES)
    tokens = P(AXES, None)
    rows = P(("zh", "y", "c"), None)
    return jax.shard_map(
        shards,
        mesh=fine,
        in_specs=(tokens, tokens, rows, rows),
        out_specs=(tokens, P(("zh", "y", "c", "x", "zl"), None)),
        check_vma=False,
    )
```

```python
import functools
import math

import jax
import jax.numpy as jnp
from jax import lax
from jax.experimental import pallas as pl
from jax.experimental.pallas import tpu as pltpu
from jax.sharding import Mesh
from jax.sharding import PartitionSpec as P

BLOCK = 128
NX, NZL, NZH, NY, NC = 4, 8, 2, 4, 2
NZ = NZL * NZH
AXES = ("x", "zl", "zh", "y", "c")
MIB = 1024 * 1024
AHEAD = 3
LEFT = 768
CHAIN = 16 * 10**9


def shift(value, axis, step):
    size = lax.axis_size(axis)
    return lax.ppermute(value, axis, [(i, (i + step) % size) for i in range(size)])


def chip_shift(value, move):
    def index(x, z, y, c):
        return (((x * NZL + z % NZL) * NZH + z // NZL) * NY + y) * NC + c

    pairs = []
    for x in range(NX):
        for z in range(NZ):
            to_x, to_z = move(x, z)
            for y in range(NY):
                for c in range(NC):
                    pairs.append((index(x, z, y, c), index(to_x, to_z, y, c)))
    return lax.ppermute(value, AXES, pairs)


def total_of(parts, dtype):
    total = parts[0].astype(jnp.float32)
    for part in parts[1:]:
        total = total + part.astype(jnp.float32)
    return total.astype(dtype)


def weight_kernel(odd, quant, scales, weight, half):
    rows, columns = quant.shape
    levels = quant[...].astype(jnp.float32)
    factors = scales[...].T
    for block in range(columns // BLOCK):
        run = slice(block * BLOCK, (block + 1) * BLOCK)
        weight[:, run] = (levels[:, run] * factors[:, block : block + 1]).astype(weight.dtype)
    part = half.shape[0]
    half[...] = weight[pl.ds(pl.multiple_of(odd[0] * part, part), part), :]


def weights(odd, quant, scales):
    rows, columns = quant.shape
    vmem = pl.BlockSpec(memory_space=pltpu.VMEM)
    quant, scales = (
        pltpu.with_memory_space_constraint(v, pltpu.HBM) for v in (quant, scales.T)
    )
    return pl.pallas_call(
        weight_kernel,
        out_shape=[
            jax.ShapeDtypeStruct((rows, columns), jnp.bfloat16),
            jax.ShapeDtypeStruct((rows // 2, columns), jnp.bfloat16),
        ],
        in_specs=[pl.BlockSpec(memory_space=pltpu.SMEM), vmem, vmem],
        out_specs=[vmem, vmem],
        compiler_params=pltpu.CompilerParams(vmem_limit_bytes=8 * MIB),
        cost_estimate=pl.CostEstimate(
            flops=rows * columns, bytes_accessed=4 * rows * columns, transcendentals=0
        ),
        name="weights",
    )(odd, quant, scales)


def partial_kernel(
    factor, where, acts, acts_in, grads, grads_in, left, r0, r1, r2, r3, *scratch
):
    lhs, rhs, lbuf, rbuf, in_sems, out_sems = scratch
    tokens = acts.shape[0]
    steps = lhs.shape[0]
    each = NY * NZH // steps
    _, _, rows, cut = left.shape
    span = rows * NX
    core, x, y = where[0], where[1], where[2]
    row_group = [lax.rem(k + NX - x, NX) for k in range(NX)]

    first = [
        pltpu.make_async_copy(
            source, rhs.at[pl.ds(half * tokens, tokens)], in_sems.at[2 * NY * NZH + half]
        )
        for half, source in enumerate((grads, grads_in))
    ]
    for copy in first:
        copy.start()
    loads = []
    for j in range(NY * NZH):
        block = j % NZH * NY + lax.rem(y + j // NZH, NY)
        start = pl.multiple_of((block * NC + core) * span, span)
        for half, source in enumerate((acts, acts_in)):
            loads.append(
                pltpu.make_async_copy(
                    source.at[:, pl.ds(start, span)],
                    lhs.at[j // each, pl.ds(half * tokens, tokens), pl.ds(j % each * span, span)],
                    in_sems.at[2 * j + half],
                )
            )
            loads[-1].start()
    for copy in first:
        copy.wait()
    stores = []
    for step in range(steps):
        for copy in loads[2 * each * step : 2 * each * (step + 1)]:
            copy.wait()
        value = lax.dot_general(
            lhs[step], rhs[...], (((0,), (0,)), ((), ())), preferred_element_type=jnp.float32
        )
        value = (value * factor).astype(left.dtype)
        for t in range(each):
            j = step * each + t
            k, z_hi = j // NZH, j % NZH
            for group in range(NX):
                start = t * span + group * rows
                lbuf[j, group] = value[start : start + rows, :cut]
                rbuf[k, row_group[group] * NZH + z_hi] = value[start : start + rows, cut:]
            place = lax.rem(y + k, NY) * NZH + z_hi
            stores.append(
                pltpu.make_async_copy(lbuf.at[j], left.at[:, place], out_sems.at[NY + j])
            )
            stores[-1].start()
            if z_hi == NZH - 1:
                stores.append(
                    pltpu.make_async_copy(rbuf.at[k], (r0, r1, r2, r3)[k], out_sems.at[k])
                )
                stores[-1].start()
    for copy in stores:
        copy.wait()


def partials(where, acts, acts_in, grads, grads_in, factor):
    tokens, width = acts.shape
    columns = grads.shape[1]
    blocks = NZH * NY
    span = width // (blocks * NC)
    rows = span // NX
    steps = 2
    cut = LEFT
    acts, grads = (pltpu.with_memory_space_constraint(v, pltpu.HBM) for v in (acts, grads))
    anywhere = pl.BlockSpec(memory_space=pl.ANY)
    right = (NX * NZH, rows, columns - cut)
    return pl.pallas_call(
        functools.partial(partial_kernel, factor),
        out_shape=[pltpu.HBM((NX, blocks, rows, cut), jnp.bfloat16)]
        + [pltpu.HBM(right, jnp.bfloat16)] * NY,
        in_specs=[pl.BlockSpec(memory_space=pltpu.SMEM)] + [anywhere] * 4,
        out_specs=[anywhere] * (1 + NY),
        scratch_shapes=[
            pltpu.VMEM((steps, 2 * tokens, blocks // steps * span), jnp.bfloat16),
            pltpu.VMEM((2 * tokens, columns), jnp.bfloat16),
            pltpu.VMEM((blocks, NX, rows, cut), jnp.bfloat16),
            pltpu.VMEM((NY, *right), jnp.bfloat16),
            pltpu.SemaphoreType.DMA((2 * blocks + 2,)),
            pltpu.SemaphoreType.DMA((blocks + NY,)),
        ],
        compiler_params=pltpu.CompilerParams(vmem_limit_bytes=24 * MIB),
        cost_estimate=pl.CostEstimate(
            flops=4 * tokens * columns * span * blocks,
            bytes_accessed=2 * blocks * span * columns + 4 * tokens * width,
            transcendentals=0,
        ),
        name="partials",
    )(where, acts, acts_in, grads, grads_in)


def left_kernel(parts, out, held, sems):
    pieces, terms, rows, columns = held.shape
    copies = [
        pltpu.make_async_copy(parts.at[:, pl.ds(q * rows, rows)], held.at[q], sems.at[q])
        for q in range(pieces)
    ]
    for copy in copies[:AHEAD]:
        copy.start()
    for q, copy in enumerate(copies):
        if q + AHEAD < pieces:
            copies[q + AHEAD].start()
        copy.wait()
        out[q * rows : (q + 1) * rows] = total_of([held[q, k] for k in range(terms)], out.dtype)


def left_sums(parts):
    terms, rows, columns = parts.shape
    pieces = 4
    return pl.pallas_call(
        left_kernel,
        out_shape=jax.ShapeDtypeStruct((rows, columns), parts.dtype),
        in_specs=[pl.BlockSpec(memory_space=pl.ANY)],
        out_specs=pl.BlockSpec(memory_space=pltpu.VMEM),
        scratch_shapes=[
            pltpu.VMEM((pieces, terms, rows // pieces, columns), parts.dtype),
            pltpu.SemaphoreType.DMA((pieces,)),
        ],
        compiler_params=pltpu.CompilerParams(vmem_limit_bytes=16 * MIB),
        cost_estimate=pl.CostEstimate(
            flops=CHAIN, bytes_accessed=2 * terms * rows * columns, transcendentals=0
        ),
        name="left_sums",
    )(parts)


def right_kernel(*refs):
    count = len(refs) // 2
    parts, outs = refs[:count], refs[count:]
    rows = outs[0].shape[0]
    for k, out in enumerate(outs):
        run = slice(k * rows, (k + 1) * rows)
        out[...] = total_of([part[run] for part in parts], out.dtype)


def right_sums(parts):
    rows, columns = parts[0].shape
    vmem = pl.BlockSpec(memory_space=pltpu.VMEM)
    count = len(parts)
    return pl.pallas_call(
        right_kernel,
        out_shape=[jax.ShapeDtypeStruct((rows // count, columns), parts[0].dtype)] * count,
        in_specs=[vmem] * count,
        out_specs=[vmem] * count,
        compiler_params=pltpu.CompilerParams(vmem_limit_bytes=16 * MIB),
        cost_estimate=pl.CostEstimate(
            flops=CHAIN, bytes_accessed=2 * count * rows * columns, transcendentals=0
        ),
        name="right_sums",
    )(*parts)


def joined_kernel(left, *refs):
    parts, out = refs[:-1], refs[-1]
    cut = left.shape[2]
    out[:, :cut] = total_of([left[k] for k in range(left.shape[0])], out.dtype)
    out[:, cut:] = total_of([part[...] for part in parts], out.dtype)


def joined_sums(left, parts):
    _, rows, cut = left.shape
    vmem = pl.BlockSpec(memory_space=pltpu.VMEM)
    return pl.pallas_call(
        joined_kernel,
        out_shape=jax.ShapeDtypeStruct((rows, cut + parts[0].shape[1]), left.dtype),
        in_specs=[vmem] * (1 + len(parts)),
        out_specs=vmem,
        compiler_params=pltpu.CompilerParams(vmem_limit_bytes=16 * MIB),
        cost_estimate=pl.CostEstimate(
            flops=CHAIN, bytes_accessed=10 * rows * 1024, transcendentals=0
        ),
        name="joined_sums",
    )(left, *parts)


def input_kernel(where, grads, weight, *rest):
    out, held, lhs, result, in_sems, out_sems = rest[-6:]
    groups, rows, _ = held.shape
    first = pltpu.make_async_copy(grads, lhs, in_sems.at[2 * groups])
    first.start()
    half = rows // 2
    copies = []
    for group in range(groups):
        copies.append(
            [
                pltpu.make_async_copy(
                    weight.at[group, pl.ds(i * half, half)],
                    held.at[group, pl.ds(pl.multiple_of((where[1] ^ i) * half, half), half)],
                    in_sems.at[2 * group + i],
                )
                for i in range(2)
            ]
        )
    for pair in copies[:AHEAD]:
        for copy in pair:
            copy.start()
    first.wait()
    done = []
    for group, pair in enumerate(copies):
        if group + AHEAD < groups:
            for copy in copies[group + AHEAD]:
                copy.start()
        for copy in pair:
            copy.wait()
        run = pl.ds(group * rows, rows)
        result[:, run] = lax.dot_general(
            lhs[...], held[group], (((1,), (1,)), ((), ())), preferred_element_type=jnp.float32
        ).astype(result.dtype)
        start = pl.multiple_of((where[0] + group) * rows, rows)
        done.append(
            pltpu.make_async_copy(
                result.at[:, run], out.at[:, pl.ds(start, rows)], out_sems.at[group]
            )
        )
        done[-1].start()
    for copy in done:
        copy.wait()


def input_part(place, turn, grads, weight, width, before=None):
    tokens, columns = grads.shape
    groups, rows, _ = weight.shape
    weight = pltpu.with_memory_space_constraint(weight, pltpu.HBM)
    args = [jnp.stack([place, turn]).astype(jnp.int32), grads, weight]
    aliases = {}
    if before is not None:
        args.append(before)
        aliases = {3: 0}
    anywhere = pl.BlockSpec(memory_space=pl.ANY)
    return pl.pallas_call(
        input_kernel,
        out_shape=jax.ShapeDtypeStruct((tokens, width), jnp.bfloat16),
        in_specs=[pl.BlockSpec(memory_space=pltpu.SMEM)] + [anywhere] * (len(args) - 1),
        out_specs=anywhere,
        scratch_shapes=[
            pltpu.VMEM((groups, rows, columns), jnp.bfloat16),
            pltpu.VMEM((tokens, columns), jnp.bfloat16),
            pltpu.VMEM((tokens, groups * rows), jnp.bfloat16),
            pltpu.SemaphoreType.DMA((2 * groups + 1,)),
            pltpu.SemaphoreType.DMA((groups,)),
        ],
        input_output_aliases=aliases,
        compiler_params=pltpu.CompilerParams(vmem_limit_bytes=16 * MIB),
        cost_estimate=pl.CostEstimate(
            flops=2 * tokens * columns * groups * rows,
            bytes_accessed=2 * groups * rows * columns + 4 * tokens * columns,
            transcendentals=0,
        ),
        name="input_part",
    )(*args)


def shards(acts, grads_out, quant, scales):
    tokens, width = acts.shape
    columns = grads_out.shape[1]
    shard_rows = quant.shape[0]
    total_tokens = tokens * lax.axis_size(AXES)
    x, zl, zh, y, c = (lax.axis_index(name) for name in AXES)
    odd = zl % 2
    groups = NY * NC
    chunk = NZH * NZL * 8

    acts_in = shift(acts, "c", 1)
    grads_in = shift(grads_out, "c", 1)
    weight, piece = weights(odd[None].astype(jnp.int32), quant, scales)
    own_half = lax.all_gather(weight, ("y", "c"), axis=0, tiled=True)
    fetched = chip_shift(piece, lambda i, z: (i, (z + NZL) % NZ))

    factor = 1.0 / math.sqrt(total_tokens)
    where = jnp.stack([c, x, y]).astype(jnp.int32)
    where, _ = lax.optimization_barrier((where, weight))
    left, *right = partials(where, acts, acts_in, grads_out, grads_in, factor)
    left = lax.all_to_all(left, "x", split_axis=0, concat_axis=0, tiled=True)
    right = [right[0]] + [shift(right[k], "y", k) for k in (1, 3, 2)]

    swapped = chip_shift(fetched, lambda i, z: (i, z ^ 1))
    other_half = lax.all_gather(
        jnp.concatenate([fetched, swapped], axis=0), ("y", "c"), axis=0, tiled=True
    )

    left = left_sums(left.reshape(NX, NY * chunk, LEFT)).reshape(NY, chunk, LEFT)
    right = right_sums([part.reshape(NX * chunk, columns - LEFT) for part in right])
    grads_later, _ = lax.optimization_barrier((grads_out, left))
    left = lax.all_to_all(left, "y", split_axis=0, concat_axis=0, tiled=True)
    right = [right[0]] + [shift(right[k], "x", k) for k in (1, 3, 2)]
    own_half = own_half.reshape(groups, shard_rows, columns)
    grad_input = input_part(zh * groups, 0 * odd, grads_later, own_half, width)
    grad_input, left = lax.optimization_barrier((grad_input, left))
    rows = joined_sums(left, right).reshape(NZ, 8, columns)
    rows = lax.all_to_all(rows, ("zh", "zl"), split_axis=0, concat_axis=0, tiled=True)
    other_half = other_half.reshape(groups, shard_rows, columns)
    grad_input = input_part(
        (1 - zh) * groups, odd, grads_later, other_half, width, grad_input
    )
    grad_input, rows = lax.optimization_barrier((grad_input, rows))
    weight_grad = jnp.sum(rows, axis=0, dtype=jnp.float32)
    return (grad_input, weight_grad)


def solution(mesh):
    fine = Mesh(mesh.devices.reshape(NX, NZL, NZH, NY, NC), AXES)
    tokens = P(AXES, None)
    rows = P(("zh", "y", "c"), None)
    return jax.shard_map(
        shards,
        mesh=fine,
        in_specs=(tokens, tokens, rows, rows),
        out_specs=(tokens, P(("zh", "y", "c", "x", "zl"), None)),
        check_vma=False,
    )
```

```python
import functools
import math

import jax
import jax.numpy as jnp
from jax import lax
from jax.experimental import pallas as pl
from jax.experimental.pallas import tpu as pltpu
from jax.sharding import Mesh
from jax.sharding import PartitionSpec as P

BLOCK = 128
NX, NZL, NZH, NY, NC = 4, 8, 2, 4, 2
NZ = NZL * NZH
AXES = ("x", "zl", "zh", "y", "c")
MIB = 1024 * 1024
AHEAD = 3
LEFT = 768
CHAIN = 16 * 10**9


def shift(value, axis, step):
    size = lax.axis_size(axis)
    return lax.ppermute(value, axis, [(i, (i + step) % size) for i in range(size)])


def chip_shift(value, move):
    def index(x, z, y, c):
        return (((x * NZL + z % NZL) * NZH + z // NZL) * NY + y) * NC + c

    pairs = []
    for x in range(NX):
        for z in range(NZ):
            to_x, to_z = move(x, z)
            for y in range(NY):
                for c in range(NC):
                    pairs.append((index(x, z, y, c), index(to_x, to_z, y, c)))
    return lax.ppermute(value, AXES, pairs)


def total_of(parts, dtype):
    total = parts[0].astype(jnp.float32)
    for part in parts[1:]:
        total = total + part.astype(jnp.float32)
    return total.astype(dtype)


def weight_kernel(odd, quant, scales, weight, half):
    rows, columns = quant.shape
    levels = quant[...].astype(jnp.float32)
    factors = scales[...].T
    for block in range(columns // BLOCK):
        run = slice(block * BLOCK, (block + 1) * BLOCK)
        weight[:, run] = (levels[:, run] * factors[:, block : block + 1]).astype(weight.dtype)
    part = half.shape[0]
    half[...] = weight[pl.ds(pl.multiple_of(odd[0] * part, part), part), :]


def weights(odd, quant, scales):
    rows, columns = quant.shape
    vmem = pl.BlockSpec(memory_space=pltpu.VMEM)
    quant, scales = (
        pltpu.with_memory_space_constraint(v, pltpu.HBM) for v in (quant, scales.T)
    )
    return pl.pallas_call(
        weight_kernel,
        out_shape=[
            jax.ShapeDtypeStruct((rows, columns), jnp.bfloat16),
            jax.ShapeDtypeStruct((rows // 2, columns), jnp.bfloat16),
        ],
        in_specs=[pl.BlockSpec(memory_space=pltpu.SMEM), vmem, vmem],
        out_specs=[vmem, vmem],
        compiler_params=pltpu.CompilerParams(vmem_limit_bytes=8 * MIB),
        cost_estimate=pl.CostEstimate(
            flops=rows * columns, bytes_accessed=4 * rows * columns, transcendentals=0
        ),
        name="weights",
    )(odd, quant, scales)


def partial_kernel(
    factor, where, acts, acts_in, grads, grads_in, left, r0, r1, r2, r3, *scratch
):
    lhs, rhs, lbuf, rbuf, in_sems, out_sems = scratch
    tokens = acts.shape[0]
    steps = lhs.shape[0]
    each = NY * NZH // steps
    _, _, rows, cut = left.shape
    span = rows * NX
    core, x, y = where[0], where[1], where[2]
    row_group = [lax.rem(k + NX - x, NX) for k in range(NX)]

    first = [
        pltpu.make_async_copy(
            source, rhs.at[pl.ds(half * tokens, tokens)], in_sems.at[2 * NY * NZH + half]
        )
        for half, source in enumerate((grads, grads_in))
    ]
    for copy in first:
        copy.start()
    loads = []
    for j in range(NY * NZH):
        block = j % NZH * NY + lax.rem(y + j // NZH, NY)
        start = pl.multiple_of((block * NC + core) * span, span)
        for half, source in enumerate((acts, acts_in)):
            loads.append(
                pltpu.make_async_copy(
                    source.at[:, pl.ds(start, span)],
                    lhs.at[j // each, pl.ds(half * tokens, tokens), pl.ds(j % each * span, span)],
                    in_sems.at[2 * j + half],
                )
            )
            loads[-1].start()
    for copy in first:
        copy.wait()
    stores = []
    for step in range(steps):
        for copy in loads[2 * each * step : 2 * each * (step + 1)]:
            copy.wait()
        value = lax.dot_general(
            lhs[step], rhs[...], (((0,), (0,)), ((), ())), preferred_element_type=jnp.float32
        )
        value = (value * factor).astype(left.dtype)
        for t in range(each):
            j = step * each + t
            k, z_hi = j // NZH, j % NZH
            for group in range(NX):
                start = t * span + group * rows
                lbuf[j, group] = value[start : start + rows, :cut]
                rbuf[k, row_group[group] * NZH + z_hi] = value[start : start + rows, cut:]
            place = lax.rem(y + k, NY) * NZH + z_hi
            stores.append(
                pltpu.make_async_copy(lbuf.at[j], left.at[:, place], out_sems.at[NY + j])
            )
            stores[-1].start()
            if z_hi == NZH - 1:
                stores.append(
                    pltpu.make_async_copy(rbuf.at[k], (r0, r1, r2, r3)[k], out_sems.at[k])
                )
                stores[-1].start()
    for copy in stores:
        copy.wait()


def partials(where, acts, acts_in, grads, grads_in, factor):
    tokens, width = acts.shape
    columns = grads.shape[1]
    blocks = NZH * NY
    span = width // (blocks * NC)
    rows = span // NX
    steps = 2
    cut = LEFT
    acts, grads = (pltpu.with_memory_space_constraint(v, pltpu.HBM) for v in (acts, grads))
    anywhere = pl.BlockSpec(memory_space=pl.ANY)
    right = (NX * NZH, rows, columns - cut)
    return pl.pallas_call(
        functools.partial(partial_kernel, factor),
        out_shape=[pltpu.HBM((NX, blocks, rows, cut), jnp.bfloat16)]
        + [pltpu.HBM(right, jnp.bfloat16)] * NY,
        in_specs=[pl.BlockSpec(memory_space=pltpu.SMEM)] + [anywhere] * 4,
        out_specs=[anywhere] * (1 + NY),
        scratch_shapes=[
            pltpu.VMEM((steps, 2 * tokens, blocks // steps * span), jnp.bfloat16),
            pltpu.VMEM((2 * tokens, columns), jnp.bfloat16),
            pltpu.VMEM((blocks, NX, rows, cut), jnp.bfloat16),
            pltpu.VMEM((NY, *right), jnp.bfloat16),
            pltpu.SemaphoreType.DMA((2 * blocks + 2,)),
            pltpu.SemaphoreType.DMA((blocks + NY,)),
        ],
        compiler_params=pltpu.CompilerParams(vmem_limit_bytes=24 * MIB),
        cost_estimate=pl.CostEstimate(
            flops=4 * tokens * columns * span * blocks,
            bytes_accessed=2 * blocks * span * columns + 4 * tokens * width,
            transcendentals=0,
        ),
        name="partials",
    )(where, acts, acts_in, grads, grads_in)


def left_kernel(parts, out, held, result, sems, out_sems):
    pieces, terms, rows, columns = held.shape
    stores = []
    copies = [
        pltpu.make_async_copy(parts.at[:, pl.ds(q * rows, rows)], held.at[q], sems.at[q])
        for q in range(pieces)
    ]
    for copy in copies[:AHEAD]:
        copy.start()
    for q, copy in enumerate(copies):
        if q + AHEAD < pieces:
            copies[q + AHEAD].start()
        copy.wait()
        result[q] = total_of([held[q, k] for k in range(terms)], out.dtype)
        stores.append(
            pltpu.make_async_copy(result.at[q], out.at[pl.ds(q * rows, rows)], out_sems.at[q])
        )
        stores[-1].start()
    for copy in stores:
        copy.wait()


def left_sums(parts):
    terms, rows, columns = parts.shape
    pieces = 4
    return pl.pallas_call(
        left_kernel,
        out_shape=pltpu.HBM((rows, columns), parts.dtype),
        in_specs=[pl.BlockSpec(memory_space=pl.ANY)],
        out_specs=pl.BlockSpec(memory_space=pl.ANY),
        scratch_shapes=[
            pltpu.VMEM((pieces, terms, rows // pieces, columns), parts.dtype),
            pltpu.VMEM((pieces, rows // pieces, columns), parts.dtype),
            pltpu.SemaphoreType.DMA((pieces,)),
            pltpu.SemaphoreType.DMA((pieces,)),
        ],
        compiler_params=pltpu.CompilerParams(vmem_limit_bytes=16 * MIB),
        cost_estimate=pl.CostEstimate(
            flops=CHAIN, bytes_accessed=2 * terms * rows * columns, transcendentals=0
        ),
        name="left_sums",
    )(parts)


def right_kernel(*refs):
    held, sems = refs[-2:]
    count = held.shape[0]
    parts, outs = refs[:count], refs[count:-2]
    rows = outs[0].shape[0]
    copies = [
        pltpu.make_async_copy(part, held.at[k], sems.at[k]) for k, part in enumerate(parts)
    ]
    for copy in copies:
        copy.start()
    for copy in copies:
        copy.wait()
    for k, out in enumerate(outs):
        run = slice(k * rows, (k + 1) * rows)
        out[...] = total_of([held[i, run] for i in range(count)], out.dtype)


def right_sums(parts):
    rows, columns = parts[0].shape
    count = len(parts)
    return pl.pallas_call(
        right_kernel,
        out_shape=[jax.ShapeDtypeStruct((rows // count, columns), parts[0].dtype)] * count,
        in_specs=[pl.BlockSpec(memory_space=pl.ANY)] * count,
        out_specs=[pl.BlockSpec(memory_space=pltpu.VMEM)] * count,
        scratch_shapes=[
            pltpu.VMEM((count, rows, columns), parts[0].dtype),
            pltpu.SemaphoreType.DMA((count,)),
        ],
        compiler_params=pltpu.CompilerParams(vmem_limit_bytes=16 * MIB),
        cost_estimate=pl.CostEstimate(
            flops=CHAIN, bytes_accessed=2 * count * rows * columns, transcendentals=0
        ),
        name="right_sums",
    )(*parts)


def joined_kernel(left, *refs):
    parts, out = refs[:-1], refs[-1]
    cut = left.shape[2]
    out[:, :cut] = total_of([left[k] for k in range(left.shape[0])], out.dtype)
    out[:, cut:] = total_of([part[...] for part in parts], out.dtype)


def joined_sums(left, parts):
    _, rows, cut = left.shape
    vmem = pl.BlockSpec(memory_space=pltpu.VMEM)
    return pl.pallas_call(
        joined_kernel,
        out_shape=jax.ShapeDtypeStruct((rows, cut + parts[0].shape[1]), left.dtype),
        in_specs=[vmem] * (1 + len(parts)),
        out_specs=vmem,
        compiler_params=pltpu.CompilerParams(vmem_limit_bytes=16 * MIB),
        cost_estimate=pl.CostEstimate(
            flops=CHAIN, bytes_accessed=10 * rows * 1024, transcendentals=0
        ),
        name="joined_sums",
    )(left, *parts)


def input_kernel(where, grads, weight, *rest):
    out, held, lhs, result, in_sems, out_sems = rest[-6:]
    groups, rows, _ = held.shape
    first = pltpu.make_async_copy(grads, lhs, in_sems.at[2 * groups])
    first.start()
    half = rows // 2
    copies = []
    for group in range(groups):
        copies.append(
            [
                pltpu.make_async_copy(
                    weight.at[group, pl.ds(i * half, half)],
                    held.at[group, pl.ds(pl.multiple_of((where[1] ^ i) * half, half), half)],
                    in_sems.at[2 * group + i],
                )
                for i in range(2)
            ]
        )
    for pair in copies[:AHEAD]:
        for copy in pair:
            copy.start()
    first.wait()
    done = []
    for group, pair in enumerate(copies):
        if group + AHEAD < groups:
            for copy in copies[group + AHEAD]:
                copy.start()
        for copy in pair:
            copy.wait()
        run = pl.ds(group * rows, rows)
        result[:, run] = lax.dot_general(
            lhs[...], held[group], (((1,), (1,)), ((), ())), preferred_element_type=jnp.float32
        ).astype(result.dtype)
        start = pl.multiple_of((where[0] + group) * rows, rows)
        done.append(
            pltpu.make_async_copy(
                result.at[:, run], out.at[:, pl.ds(start, rows)], out_sems.at[group]
            )
        )
        done[-1].start()
    for copy in done:
        copy.wait()


def input_part(place, turn, grads, weight, width, before=None):
    tokens, columns = grads.shape
    groups, rows, _ = weight.shape
    weight = pltpu.with_memory_space_constraint(weight, pltpu.HBM)
    args = [jnp.stack([place, turn]).astype(jnp.int32), grads, weight]
    aliases = {}
    if before is not None:
        args.append(before)
        aliases = {3: 0}
    anywhere = pl.BlockSpec(memory_space=pl.ANY)
    return pl.pallas_call(
        input_kernel,
        out_shape=jax.ShapeDtypeStruct((tokens, width), jnp.bfloat16),
        in_specs=[pl.BlockSpec(memory_space=pltpu.SMEM)] + [anywhere] * (len(args) - 1),
        out_specs=anywhere,
        scratch_shapes=[
            pltpu.VMEM((groups, rows, columns), jnp.bfloat16),
            pltpu.VMEM((tokens, columns), jnp.bfloat16),
            pltpu.VMEM((tokens, groups * rows), jnp.bfloat16),
            pltpu.SemaphoreType.DMA((2 * groups + 1,)),
            pltpu.SemaphoreType.DMA((groups,)),
        ],
        input_output_aliases=aliases,
        compiler_params=pltpu.CompilerParams(vmem_limit_bytes=16 * MIB),
        cost_estimate=pl.CostEstimate(
            flops=2 * tokens * columns * groups * rows,
            bytes_accessed=2 * groups * rows * columns + 4 * tokens * columns,
            transcendentals=0,
        ),
        name="input_part",
    )(*args)


def shards(acts, grads_out, quant, scales):
    tokens, width = acts.shape
    columns = grads_out.shape[1]
    shard_rows = quant.shape[0]
    total_tokens = tokens * lax.axis_size(AXES)
    x, zl, zh, y, c = (lax.axis_index(name) for name in AXES)
    odd = zl % 2
    groups = NY * NC
    chunk = NZH * NZL * 8

    acts_in = shift(acts, "c", 1)
    grads_in = shift(grads_out, "c", 1)
    weight, piece = weights(odd[None].astype(jnp.int32), quant, scales)
    own_half = lax.all_gather(weight, ("y", "c"), axis=0, tiled=True)
    fetched = chip_shift(piece, lambda i, z: (i, (z + NZL) % NZ))

    factor = 1.0 / math.sqrt(total_tokens)
    where = jnp.stack([c, x, y]).astype(jnp.int32)
    where, _ = lax.optimization_barrier((where, weight))
    left, *right = partials(where, acts, acts_in, grads_out, grads_in, factor)
    left = lax.all_to_all(left, "x", split_axis=0, concat_axis=0, tiled=True)
    right = [right[0]] + [shift(right[k], "y", k) for k in (1, 3, 2)]

    swapped = chip_shift(fetched, lambda i, z: (i, z ^ 1))
    both = jnp.concatenate([fetched, swapped], axis=0)
    both, *_ = lax.optimization_barrier((both, right[1], right[2]))
    other_half = lax.all_gather(both, ("y", "c"), axis=0, tiled=True)

    right = right_sums([part.reshape(NX * chunk, columns - LEFT) for part in right])
    left = left_sums(left.reshape(NX, NY * chunk, LEFT)).reshape(NY, chunk, LEFT)
    left = lax.all_to_all(left, "y", split_axis=0, concat_axis=0, tiled=True)
    right = [right[0]] + [shift(right[k], "x", k) for k in (1, 3, 2)]
    rows = joined_sums(left, right).reshape(NZ, 8, columns)
    grads_later, _ = lax.optimization_barrier((grads_out, rows))
    rows = lax.all_to_all(rows, ("zh", "zl"), split_axis=0, concat_axis=0, tiled=True)
    own_half = own_half.reshape(groups, shard_rows, columns)
    grad_input = input_part(zh * groups, 0 * odd, grads_later, own_half, width)
    other_half = other_half.reshape(groups, shard_rows, columns)
    grad_input = input_part(
        (1 - zh) * groups, odd, grads_later, other_half, width, grad_input
    )
    grad_input, rows = lax.optimization_barrier((grad_input, rows))
    weight_grad = jnp.sum(rows, axis=0, dtype=jnp.float32)
    return (grad_input, weight_grad)


def solution(mesh):
    fine = Mesh(mesh.devices.reshape(NX, NZL, NZH, NY, NC), AXES)
    tokens = P(AXES, None)
    rows = P(("zh", "y", "c"), None)
    return jax.shard_map(
        shards,
        mesh=fine,
        in_specs=(tokens, tokens, rows, rows),
        out_specs=(tokens, P(("zh", "y", "c", "x", "zl"), None)),
        check_vma=False,
    )
```

```python
import functools
import math

import jax
import jax.numpy as jnp
from jax import lax
from jax.experimental import pallas as pl
from jax.experimental.pallas import tpu as pltpu
from jax.sharding import Mesh
from jax.sharding import PartitionSpec as P

BLOCK = 128
NX, NZL, NZH, NY, NC = 4, 8, 2, 4, 2
NZ = NZL * NZH
AXES = ("x", "zl", "zh", "y", "c")
MIB = 1024 * 1024
AHEAD = 3
CHAIN = 320 * 10**8


def shift(value, axis, step):
    size = lax.axis_size(axis)
    return lax.ppermute(value, axis, [(i, (i + step) % size) for i in range(size)])


def chip_shift(value, move):
    def index(x, z, y, c):
        return (((x * NZL + z % NZL) * NZH + z // NZL) * NY + y) * NC + c

    pairs = []
    for x in range(NX):
        for z in range(NZ):
            to_x, to_z = move(x, z)
            for y in range(NY):
                for c in range(NC):
                    pairs.append((index(x, z, y, c), index(to_x, to_z, y, c)))
    return lax.ppermute(value, AXES, pairs)


def total_of(parts, dtype):
    total = parts[0].astype(jnp.float32)
    for part in parts[1:]:
        total = total + part.astype(jnp.float32)
    return total.astype(dtype)


def weight_kernel(odd, quant, scales, weight, half):
    rows, columns = quant.shape
    levels = quant[...].astype(jnp.float32)
    factors = scales[...].T
    for block in range(columns // BLOCK):
        run = slice(block * BLOCK, (block + 1) * BLOCK)
        weight[:, run] = (levels[:, run] * factors[:, block : block + 1]).astype(weight.dtype)
    part = half.shape[0]
    half[...] = weight[pl.ds(pl.multiple_of(odd[0] * part, part), part), :]


def weights(odd, quant, scales):
    rows, columns = quant.shape
    vmem = pl.BlockSpec(memory_space=pltpu.VMEM)
    quant, scales = (
        pltpu.with_memory_space_constraint(v, pltpu.HBM) for v in (quant, scales.T)
    )
    return pl.pallas_call(
        weight_kernel,
        out_shape=[
            jax.ShapeDtypeStruct((rows, columns), jnp.bfloat16),
            jax.ShapeDtypeStruct((rows // 2, columns), jnp.bfloat16),
        ],
        in_specs=[pl.BlockSpec(memory_space=pltpu.SMEM), vmem, vmem],
        out_specs=[vmem, vmem],
        compiler_params=pltpu.CompilerParams(vmem_limit_bytes=8 * MIB),
        cost_estimate=pl.CostEstimate(
            flops=rows * columns, bytes_accessed=4 * rows * columns, transcendentals=0
        ),
        name="weights",
    )(odd, quant, scales)


def partial_kernel(factor, core, acts, acts_in, grads, grads_in, out, lhs, rhs, sems):
    step = pl.program_id(0)
    tokens = acts.shape[0]
    _, blocks, rows, _ = out.shape
    span = rows * NX

    def copies(at):
        found = []
        for t in range(blocks):
            j = at * blocks + t
            block = (j % NZH) * NY + j // NZH
            start = pl.multiple_of((block * NC + core[0]) * span, span)
            for half, source in enumerate((acts, acts_in)):
                found.append(
                    pltpu.make_async_copy(
                        source.at[:, pl.ds(start, span)],
                        lhs.at[at, pl.ds(half * tokens, tokens), pl.ds(t * span, span)],
                        sems.at[2 * j + half],
                    )
                )
        return found

    base = 4 * blocks
    right = [
        pltpu.make_async_copy(
            source, rhs.at[pl.ds(half * tokens, tokens)], sems.at[base + half]
        )
        for half, source in enumerate((grads, grads_in))
    ]

    @pl.when(step == 0)
    def _():
        for copy in right + copies(0) + copies(1):
            copy.start()
        for copy in right + copies(0):
            copy.wait()

    @pl.when(step == 1)
    def _():
        for copy in copies(1):
            copy.wait()

    value = lax.dot_general(
        lhs[step], rhs[...], (((0,), (0,)), ((), ())), preferred_element_type=jnp.float32
    )
    value = (value * factor).astype(out.dtype)
    for t in range(blocks):
        for x in range(NX):
            start = t * span + x * rows
            out[x, t] = value[start : start + rows]


def partials(core, acts, acts_in, grads, grads_in, factor):
    tokens, width = acts.shape
    columns = grads.shape[1]
    blocks = NZH * NY
    span = width // (blocks * NC)
    rows = span // NX
    half = blocks // 2
    acts, grads = (pltpu.with_memory_space_constraint(v, pltpu.HBM) for v in (acts, grads))
    return pl.pallas_call(
        functools.partial(partial_kernel, factor),
        out_shape=pltpu.HBM((NX, blocks, rows, columns), jnp.bfloat16),
        grid_spec=pltpu.PrefetchScalarGridSpec(
            num_scalar_prefetch=1,
            grid=(2,),
            in_specs=[pl.BlockSpec(memory_space=pl.ANY)] * 4,
            out_specs=pl.BlockSpec((NX, half, rows, columns), lambda j, core: (0, j, 0, 0)),
            scratch_shapes=[
                pltpu.VMEM((2, 2 * tokens, half * span), jnp.bfloat16),
                pltpu.VMEM((2 * tokens, columns), jnp.bfloat16),
                pltpu.SemaphoreType.DMA((2 * blocks + 2,)),
            ],
        ),
        compiler_params=pltpu.CompilerParams(vmem_limit_bytes=24 * MIB),
        cost_estimate=pl.CostEstimate(
            flops=4 * tokens * columns * span * blocks,
            bytes_accessed=2 * blocks * span * columns + 4 * tokens * width,
            transcendentals=0,
        ),
        name="partials",
    )(core, acts, acts_in, grads, grads_in)


def sum_kernel(parts, out, held, result, sems, out_sems):
    pieces, terms, rows, columns = held.shape
    stores = []
    copies = [
        pltpu.make_async_copy(parts.at[:, pl.ds(q * rows, rows)], held.at[q], sems.at[q])
        for q in range(pieces)
    ]
    for copy in copies[:AHEAD]:
        copy.start()
    for q, copy in enumerate(copies):
        if q + AHEAD < pieces:
            copies[q + AHEAD].start()
        copy.wait()
        result[q] = total_of([held[q, k] for k in range(terms)], out.dtype)
        stores.append(
            pltpu.make_async_copy(result.at[q], out.at[pl.ds(q * rows, rows)], out_sems.at[q])
        )
        stores[-1].start()
    for copy in stores:
        copy.wait()


def sums(parts):
    terms, rows, columns = parts.shape
    pieces = 4
    return pl.pallas_call(
        sum_kernel,
        out_shape=pltpu.HBM((rows, columns), parts.dtype),
        in_specs=[pl.BlockSpec(memory_space=pl.ANY)],
        out_specs=pl.BlockSpec(memory_space=pl.ANY),
        scratch_shapes=[
            pltpu.VMEM((pieces, terms, rows // pieces, columns), parts.dtype),
            pltpu.VMEM((pieces, rows // pieces, columns), parts.dtype),
            pltpu.SemaphoreType.DMA((pieces,)),
            pltpu.SemaphoreType.DMA((pieces,)),
        ],
        compiler_params=pltpu.CompilerParams(vmem_limit_bytes=16 * MIB),
        cost_estimate=pl.CostEstimate(
            flops=CHAIN, bytes_accessed=2 * terms * rows * columns, transcendentals=0
        ),
        name="sums",
    )(parts)


def input_kernel(where, grads, weight, *rest):
    out, held, lhs, result, in_sems, out_sems = rest[-6:]
    groups, rows, _ = held.shape
    first = pltpu.make_async_copy(grads, lhs, in_sems.at[2 * groups])
    first.start()
    half = rows // 2
    copies = []
    for group in range(groups):
        copies.append(
            [
                pltpu.make_async_copy(
                    weight.at[group, pl.ds(i * half, half)],
                    held.at[group, pl.ds(pl.multiple_of((where[1] ^ i) * half, half), half)],
                    in_sems.at[2 * group + i],
                )
                for i in range(2)
            ]
        )
    for pair in copies[:AHEAD]:
        for copy in pair:
            copy.start()
    first.wait()
    done = []
    for group, pair in enumerate(copies):
        if group + AHEAD < groups:
            for copy in copies[group + AHEAD]:
                copy.start()
        for copy in pair:
            copy.wait()
        run = pl.ds(group * rows, rows)
        result[:, run] = lax.dot_general(
            lhs[...], held[group], (((1,), (1,)), ((), ())), preferred_element_type=jnp.float32
        ).astype(result.dtype)
        start = pl.multiple_of((where[0] + group) * rows, rows)
        done.append(
            pltpu.make_async_copy(
                result.at[:, run], out.at[:, pl.ds(start, rows)], out_sems.at[group]
            )
        )
        done[-1].start()
    for copy in done:
        copy.wait()


def input_part(place, turn, grads, weight, width, before=None):
    tokens, columns = grads.shape
    groups, rows, _ = weight.shape
    weight = pltpu.with_memory_space_constraint(weight, pltpu.HBM)
    args = [jnp.stack([place, turn]).astype(jnp.int32), grads, weight]
    aliases = {}
    if before is not None:
        args.append(before)
        aliases = {3: 0}
    anywhere = pl.BlockSpec(memory_space=pl.ANY)
    return pl.pallas_call(
        input_kernel,
        out_shape=jax.ShapeDtypeStruct((tokens, width), jnp.bfloat16),
        in_specs=[pl.BlockSpec(memory_space=pltpu.SMEM)] + [anywhere] * (len(args) - 1),
        out_specs=anywhere,
        scratch_shapes=[
            pltpu.VMEM((groups, rows, columns), jnp.bfloat16),
            pltpu.VMEM((tokens, columns), jnp.bfloat16),
            pltpu.VMEM((tokens, groups * rows), jnp.bfloat16),
            pltpu.SemaphoreType.DMA((2 * groups + 1,)),
            pltpu.SemaphoreType.DMA((groups,)),
        ],
        input_output_aliases=aliases,
        compiler_params=pltpu.CompilerParams(vmem_limit_bytes=16 * MIB),
        cost_estimate=pl.CostEstimate(
            flops=2 * tokens * columns * groups * rows,
            bytes_accessed=2 * groups * rows * columns + 4 * tokens * columns,
            transcendentals=0,
        ),
        name="input_part",
    )(*args)


def shards(acts, grads_out, quant, scales):
    tokens, width = acts.shape
    columns = grads_out.shape[1]
    shard_rows = quant.shape[0]
    total_tokens = tokens * lax.axis_size(AXES)
    zl, zh, c = (lax.axis_index(name) for name in ("zl", "zh", "c"))
    odd = zl % 2
    groups = NY * NC
    chunk = NZH * NZL * 8

    acts_in = shift(acts, "c", 1)
    grads_in = shift(grads_out, "c", 1)
    weight, piece = weights(odd[None].astype(jnp.int32), quant, scales)
    own_half = lax.all_gather(weight, ("y", "c"), axis=0, tiled=True)
    fetched = chip_shift(piece, lambda i, z: (i, (z + NZL) % NZ))

    factor = 1.0 / math.sqrt(total_tokens)
    core = c[None].astype(jnp.int32)
    core, _ = lax.optimization_barrier((core, weight))
    parts = partials(core, acts, acts_in, grads_out, grads_in, factor)
    parts = parts.reshape(NX * NY, chunk, columns)
    received = lax.all_to_all(parts, ("x", "y"), split_axis=0, concat_axis=0, tiled=True)

    fetched, _ = lax.optimization_barrier((fetched, parts))
    swapped = chip_shift(fetched, lambda i, z: (i, z ^ 1))
    both = jnp.concatenate([fetched, swapped], axis=0)
    other_half = lax.all_gather(both, ("y", "c"), axis=0, tiled=True)
    own_half = own_half.reshape(groups, shard_rows, columns)
    grad_input = input_part(zh * groups, 0 * odd, grads_out, own_half, width)
    grad_input, received = lax.optimization_barrier((grad_input, received))
    rows = sums(received).reshape(NZ, 8, columns)
    grads_later, _ = lax.optimization_barrier((grads_out, rows))
    rows = lax.all_to_all(rows, ("zh", "zl"), split_axis=0, concat_axis=0, tiled=True)
    other_half = other_half.reshape(groups, shard_rows, columns)
    grad_input = input_part(
        (1 - zh) * groups, odd, grads_later, other_half, width, grad_input
    )
    grad_input, rows = lax.optimization_barrier((grad_input, rows))
    weight_grad = jnp.sum(rows, axis=0, dtype=jnp.float32)
    return (grad_input, weight_grad)


def solution(mesh):
    fine = Mesh(mesh.devices.reshape(NX, NZL, NZH, NY, NC), AXES)
    tokens = P(AXES, None)
    rows = P(("zh", "y", "c"), None)
    return jax.shard_map(
        shards,
        mesh=fine,
        in_specs=(tokens, tokens, rows, rows),
        out_specs=(tokens, P(("zh", "y", "c", "x", "zl"), None)),
        check_vma=False,
    )
```

```python
import functools
import math

import jax
import jax.numpy as jnp
from jax import lax
from jax.experimental import pallas as pl
from jax.experimental.pallas import tpu as pltpu
from jax.sharding import Mesh
from jax.sharding import PartitionSpec as P

BLOCK = 128
NX, NZL, NZH, NY, NC = 4, 8, 2, 4, 2
NZ = NZL * NZH
AXES = ("x", "zl", "zh", "y", "c")
MIB = 1024 * 1024
AHEAD = 3
LEFT = 768
CHAIN = 16 * 10**9


def shift(value, axis, step):
    size = lax.axis_size(axis)
    return lax.ppermute(value, axis, [(i, (i + step) % size) for i in range(size)])


def chip_shift(value, move):
    def index(x, z, y, c):
        return (((x * NZL + z % NZL) * NZH + z // NZL) * NY + y) * NC + c

    pairs = []
    for x in range(NX):
        for z in range(NZ):
            to_x, to_z = move(x, z)
            for y in range(NY):
                for c in range(NC):
                    pairs.append((index(x, z, y, c), index(to_x, to_z, y, c)))
    return lax.ppermute(value, AXES, pairs)


def total_of(parts, dtype):
    total = parts[0].astype(jnp.float32)
    for part in parts[1:]:
        total = total + part.astype(jnp.float32)
    return total.astype(dtype)


def weight_kernel(odd, quant, scales, weight, half):
    rows, columns = quant.shape
    levels = quant[...].astype(jnp.float32)
    factors = scales[...].T
    for block in range(columns // BLOCK):
        run = slice(block * BLOCK, (block + 1) * BLOCK)
        weight[:, run] = (levels[:, run] * factors[:, block : block + 1]).astype(weight.dtype)
    part = half.shape[0]
    half[...] = weight[pl.ds(pl.multiple_of(odd[0] * part, part), part), :]


def weights(odd, quant, scales):
    rows, columns = quant.shape
    vmem = pl.BlockSpec(memory_space=pltpu.VMEM)
    quant, scales = (
        pltpu.with_memory_space_constraint(v, pltpu.HBM) for v in (quant, scales.T)
    )
    return pl.pallas_call(
        weight_kernel,
        out_shape=[
            jax.ShapeDtypeStruct((rows, columns), jnp.bfloat16),
            jax.ShapeDtypeStruct((rows // 2, columns), jnp.bfloat16),
        ],
        in_specs=[pl.BlockSpec(memory_space=pltpu.SMEM), vmem, vmem],
        out_specs=[vmem, vmem],
        compiler_params=pltpu.CompilerParams(vmem_limit_bytes=8 * MIB),
        cost_estimate=pl.CostEstimate(
            flops=rows * columns, bytes_accessed=4 * rows * columns, transcendentals=0
        ),
        name="weights",
    )(odd, quant, scales)


def partial_kernel(
    factor, where, acts, acts_in, grads, grads_in, left, r0, r1, r2, r3, *scratch
):
    lhs, rhs, lbuf, rbuf, in_sems, out_sems = scratch
    tokens = acts.shape[0]
    steps = lhs.shape[0]
    each = NY * NZH // steps
    _, _, rows, cut = left.shape
    span = rows * NX
    core, x, y = where[0], where[1], where[2]
    row_group = [lax.rem(k + NX - x, NX) for k in range(NX)]

    first = [
        pltpu.make_async_copy(
            source, rhs.at[pl.ds(half * tokens, tokens)], in_sems.at[2 * NY * NZH + half]
        )
        for half, source in enumerate((grads, grads_in))
    ]
    for copy in first:
        copy.start()
    loads = []
    for j in range(NY * NZH):
        block = j % NZH * NY + lax.rem(y + j // NZH, NY)
        start = pl.multiple_of((block * NC + core) * span, span)
        for half, source in enumerate((acts, acts_in)):
            loads.append(
                pltpu.make_async_copy(
                    source.at[:, pl.ds(start, span)],
                    lhs.at[j // each, pl.ds(half * tokens, tokens), pl.ds(j % each * span, span)],
                    in_sems.at[2 * j + half],
                )
            )
            loads[-1].start()
    for copy in first:
        copy.wait()
    stores = []
    for step in range(steps):
        for copy in loads[2 * each * step : 2 * each * (step + 1)]:
            copy.wait()
        value = lax.dot_general(
            lhs[step], rhs[...], (((0,), (0,)), ((), ())), preferred_element_type=jnp.float32
        )
        value = (value * factor).astype(left.dtype)
        for t in range(each):
            j = step * each + t
            k, z_hi = j // NZH, j % NZH
            for group in range(NX):
                start = t * span + group * rows
                lbuf[j, group] = value[start : start + rows, :cut]
                rbuf[k, row_group[group] * NZH + z_hi] = value[start : start + rows, cut:]
            place = lax.rem(y + k, NY) * NZH + z_hi
            stores.append(
                pltpu.make_async_copy(lbuf.at[j], left.at[:, place], out_sems.at[NY + j])
            )
            stores[-1].start()
            if z_hi == NZH - 1:
                stores.append(
                    pltpu.make_async_copy(rbuf.at[k], (r0, r1, r2, r3)[k], out_sems.at[k])
                )
                stores[-1].start()
    for copy in stores:
        copy.wait()


def partials(where, acts, acts_in, grads, grads_in, factor):
    tokens, width = acts.shape
    columns = grads.shape[1]
    blocks = NZH * NY
    span = width // (blocks * NC)
    rows = span // NX
    steps = 2
    cut = LEFT
    acts, grads = (pltpu.with_memory_space_constraint(v, pltpu.HBM) for v in (acts, grads))
    anywhere = pl.BlockSpec(memory_space=pl.ANY)
    right = (NX * NZH, rows, columns - cut)
    return pl.pallas_call(
        functools.partial(partial_kernel, factor),
        out_shape=[pltpu.HBM((NX, blocks, rows, cut), jnp.bfloat16)]
        + [pltpu.HBM(right, jnp.bfloat16)] * NY,
        in_specs=[pl.BlockSpec(memory_space=pltpu.SMEM)] + [anywhere] * 4,
        out_specs=[anywhere] * (1 + NY),
        scratch_shapes=[
            pltpu.VMEM((steps, 2 * tokens, blocks // steps * span), jnp.bfloat16),
            pltpu.VMEM((2 * tokens, columns), jnp.bfloat16),
            pltpu.VMEM((blocks, NX, rows, cut), jnp.bfloat16),
            pltpu.VMEM((NY, *right), jnp.bfloat16),
            pltpu.SemaphoreType.DMA((2 * blocks + 2,)),
            pltpu.SemaphoreType.DMA((blocks + NY,)),
        ],
        compiler_params=pltpu.CompilerParams(vmem_limit_bytes=24 * MIB),
        cost_estimate=pl.CostEstimate(
            flops=4 * tokens * columns * span * blocks,
            bytes_accessed=2 * blocks * span * columns + 4 * tokens * width,
            transcendentals=0,
        ),
        name="partials",
    )(where, acts, acts_in, grads, grads_in)


def left_kernel(parts, out, held, result, sems, out_sems):
    pieces, terms, rows, columns = held.shape
    stores = []
    copies = [
        pltpu.make_async_copy(parts.at[:, pl.ds(q * rows, rows)], held.at[q], sems.at[q])
        for q in range(pieces)
    ]
    for copy in copies[:AHEAD]:
        copy.start()
    for q, copy in enumerate(copies):
        if q + AHEAD < pieces:
            copies[q + AHEAD].start()
        copy.wait()
        result[q] = total_of([held[q, k] for k in range(terms)], out.dtype)
        stores.append(
            pltpu.make_async_copy(result.at[q], out.at[pl.ds(q * rows, rows)], out_sems.at[q])
        )
        stores[-1].start()
    for copy in stores:
        copy.wait()


def left_sums(parts):
    terms, rows, columns = parts.shape
    pieces = 4
    return pl.pallas_call(
        left_kernel,
        out_shape=pltpu.HBM((rows, columns), parts.dtype),
        in_specs=[pl.BlockSpec(memory_space=pl.ANY)],
        out_specs=pl.BlockSpec(memory_space=pl.ANY),
        scratch_shapes=[
            pltpu.VMEM((pieces, terms, rows // pieces, columns), parts.dtype),
            pltpu.VMEM((pieces, rows // pieces, columns), parts.dtype),
            pltpu.SemaphoreType.DMA((pieces,)),
            pltpu.SemaphoreType.DMA((pieces,)),
        ],
        compiler_params=pltpu.CompilerParams(vmem_limit_bytes=16 * MIB),
        cost_estimate=pl.CostEstimate(
            flops=CHAIN, bytes_accessed=2 * terms * rows * columns, transcendentals=0
        ),
        name="left_sums",
    )(parts)


def right_kernel(*refs):
    held, sems = refs[-2:]
    count = held.shape[0]
    parts, outs = refs[:count], refs[count:-2]
    rows = outs[0].shape[0]
    copies = [
        pltpu.make_async_copy(part, held.at[k], sems.at[k]) for k, part in enumerate(parts)
    ]
    for copy in copies:
        copy.start()
    for copy in copies:
        copy.wait()
    for k, out in enumerate(outs):
        run = slice(k * rows, (k + 1) * rows)
        out[...] = total_of([held[i, run] for i in range(count)], out.dtype)


def right_sums(parts):
    rows, columns = parts[0].shape
    count = len(parts)
    parts = [pltpu.with_memory_space_constraint(parts[0], pltpu.HBM), *parts[1:]]
    return pl.pallas_call(
        right_kernel,
        out_shape=[jax.ShapeDtypeStruct((rows // count, columns), parts[0].dtype)] * count,
        in_specs=[pl.BlockSpec(memory_space=pl.ANY)] * count,
        out_specs=[pl.BlockSpec(memory_space=pltpu.VMEM)] * count,
        scratch_shapes=[
            pltpu.VMEM((count, rows, columns), parts[0].dtype),
            pltpu.SemaphoreType.DMA((count,)),
        ],
        compiler_params=pltpu.CompilerParams(vmem_limit_bytes=16 * MIB),
        cost_estimate=pl.CostEstimate(
            flops=CHAIN, bytes_accessed=2 * count * rows * columns, transcendentals=0
        ),
        name="right_sums",
    )(*parts)


def joined_kernel(left, *refs):
    parts, out = refs[:-1], refs[-1]
    cut = left.shape[2]
    out[:, :cut] = total_of([left[k] for k in range(left.shape[0])], out.dtype)
    out[:, cut:] = total_of([part[...] for part in parts], out.dtype)


def joined_sums(left, parts):
    _, rows, cut = left.shape
    vmem = pl.BlockSpec(memory_space=pltpu.VMEM)
    return pl.pallas_call(
        joined_kernel,
        out_shape=jax.ShapeDtypeStruct((rows, cut + parts[0].shape[1]), left.dtype),
        in_specs=[vmem] * (1 + len(parts)),
        out_specs=vmem,
        compiler_params=pltpu.CompilerParams(vmem_limit_bytes=16 * MIB),
        cost_estimate=pl.CostEstimate(
            flops=CHAIN, bytes_accessed=10 * rows * 1024, transcendentals=0
        ),
        name="joined_sums",
    )(left, *parts)


def input_kernel(where, grads, weight, *rest):
    out, held, lhs, result, in_sems, out_sems = rest[-6:]
    groups, rows, _ = held.shape
    first = pltpu.make_async_copy(grads, lhs, in_sems.at[2 * groups])
    first.start()
    half = rows // 2
    copies = []
    for group in range(groups):
        copies.append(
            [
                pltpu.make_async_copy(
                    weight.at[group, pl.ds(i * half, half)],
                    held.at[group, pl.ds(pl.multiple_of((where[1] ^ i) * half, half), half)],
                    in_sems.at[2 * group + i],
                )
                for i in range(2)
            ]
        )
    for pair in copies[:AHEAD]:
        for copy in pair:
            copy.start()
    first.wait()
    done = []
    for group, pair in enumerate(copies):
        if group + AHEAD < groups:
            for copy in copies[group + AHEAD]:
                copy.start()
        for copy in pair:
            copy.wait()
        run = pl.ds(group * rows, rows)
        result[:, run] = lax.dot_general(
            lhs[...], held[group], (((1,), (1,)), ((), ())), preferred_element_type=jnp.float32
        ).astype(result.dtype)
        start = pl.multiple_of((where[0] + group) * rows, rows)
        done.append(
            pltpu.make_async_copy(
                result.at[:, run], out.at[:, pl.ds(start, rows)], out_sems.at[group]
            )
        )
        done[-1].start()
    for copy in done:
        copy.wait()


def input_part(place, turn, grads, weight, width, before=None):
    tokens, columns = grads.shape
    groups, rows, _ = weight.shape
    weight = pltpu.with_memory_space_constraint(weight, pltpu.HBM)
    args = [jnp.stack([place, turn]).astype(jnp.int32), grads, weight]
    aliases = {}
    if before is not None:
        args.append(before)
        aliases = {3: 0}
    anywhere = pl.BlockSpec(memory_space=pl.ANY)
    return pl.pallas_call(
        input_kernel,
        out_shape=jax.ShapeDtypeStruct((tokens, width), jnp.bfloat16),
        in_specs=[pl.BlockSpec(memory_space=pltpu.SMEM)] + [anywhere] * (len(args) - 1),
        out_specs=anywhere,
        scratch_shapes=[
            pltpu.VMEM((groups, rows, columns), jnp.bfloat16),
            pltpu.VMEM((tokens, columns), jnp.bfloat16),
            pltpu.VMEM((tokens, groups * rows), jnp.bfloat16),
            pltpu.SemaphoreType.DMA((2 * groups + 1,)),
            pltpu.SemaphoreType.DMA((groups,)),
        ],
        input_output_aliases=aliases,
        compiler_params=pltpu.CompilerParams(vmem_limit_bytes=16 * MIB),
        cost_estimate=pl.CostEstimate(
            flops=2 * tokens * columns * groups * rows,
            bytes_accessed=2 * groups * rows * columns + 4 * tokens * columns,
            transcendentals=0,
        ),
        name="input_part",
    )(*args)


def shards(acts, grads_out, quant, scales):
    tokens, width = acts.shape
    columns = grads_out.shape[1]
    shard_rows = quant.shape[0]
    total_tokens = tokens * lax.axis_size(AXES)
    x, zl, zh, y, c = (lax.axis_index(name) for name in AXES)
    odd = zl % 2
    groups = NY * NC
    chunk = NZH * NZL * 8

    acts_in = shift(acts, "c", 1)
    grads_in = shift(grads_out, "c", 1)
    weight, piece = weights(odd[None].astype(jnp.int32), quant, scales)
    own_half = lax.all_gather(weight, ("y", "c"), axis=0, tiled=True)
    fetched = chip_shift(piece, lambda i, z: (i, (z + NZL) % NZ))

    factor = 1.0 / math.sqrt(total_tokens)
    where = jnp.stack([c, x, y]).astype(jnp.int32)
    where, _ = lax.optimization_barrier((where, weight))
    left, *right = partials(where, acts, acts_in, grads_out, grads_in, factor)
    left = lax.all_to_all(left, "x", split_axis=0, concat_axis=0, tiled=True)
    right = [right[0]] + [shift(right[k], "y", k) for k in (2, 1, 3)]

    swapped = chip_shift(fetched, lambda i, z: (i, z ^ 1))
    both = jnp.concatenate([fetched, swapped], axis=0)
    both, *_ = lax.optimization_barrier((both, *right))
    other_half = lax.all_gather(both, ("y", "c"), axis=0, tiled=True)

    right = right_sums([part.reshape(NX * chunk, columns - LEFT) for part in right])
    left = left_sums(left.reshape(NX, NY * chunk, LEFT)).reshape(NY, chunk, LEFT)
    left = lax.all_to_all(left, "y", split_axis=0, concat_axis=0, tiled=True)
    right = [right[0]] + [shift(right[k], "x", k) for k in (2, 1, 3)]
    rows = joined_sums(left, right).reshape(NZ, 8, columns)
    grads_later, _ = lax.optimization_barrier((grads_out, rows))
    rows = lax.all_to_all(rows, ("zh", "zl"), split_axis=0, concat_axis=0, tiled=True)
    own_half = own_half.reshape(groups, shard_rows, columns)
    grad_input = input_part(zh * groups, 0 * odd, grads_later, own_half, width)
    other_half = other_half.reshape(groups, shard_rows, columns)
    grad_input = input_part(
        (1 - zh) * groups, odd, grads_later, other_half, width, grad_input
    )
    grad_input, rows = lax.optimization_barrier((grad_input, rows))
    weight_grad = jnp.sum(rows, axis=0, dtype=jnp.float32)
    return (grad_input, weight_grad)


def solution(mesh):
    fine = Mesh(mesh.devices.reshape(NX, NZL, NZH, NY, NC), AXES)
    tokens = P(AXES, None)
    rows = P(("zh", "y", "c"), None)
    return jax.shard_map(
        shards,
        mesh=fine,
        in_specs=(tokens, tokens, rows, rows),
        out_specs=(tokens, P(("zh", "y", "c", "x", "zl"), None)),
        check_vma=False,
    )
```

```python
import functools
import math

import jax
import jax.numpy as jnp
from jax import lax
from jax.experimental import pallas as pl
from jax.experimental.pallas import tpu as pltpu
from jax.sharding import Mesh
from jax.sharding import PartitionSpec as P

BLOCK = 128
NX, NZL, NZH, NY, NC = 4, 8, 2, 4, 2
NZ = NZL * NZH
AXES = ("x", "zl", "zh", "y", "c")
MIB = 1024 * 1024
AHEAD = 3
LEFT = 640
CHAIN = 14 * 10**9


def shift(value, axis, step):
    size = lax.axis_size(axis)
    return lax.ppermute(value, axis, [(i, (i + step) % size) for i in range(size)])


def chip_shift(value, move):
    def index(x, z, y, c):
        return (((x * NZL + z % NZL) * NZH + z // NZL) * NY + y) * NC + c

    pairs = []
    for x in range(NX):
        for z in range(NZ):
            to_x, to_z = move(x, z)
            for y in range(NY):
                for c in range(NC):
                    pairs.append((index(x, z, y, c), index(to_x, to_z, y, c)))
    return lax.ppermute(value, AXES, pairs)


def total_of(parts, dtype):
    total = parts[0].astype(jnp.float32)
    for part in parts[1:]:
        total = total + part.astype(jnp.float32)
    return total.astype(dtype)


def weight_kernel(odd, quant, scales, weight, half):
    rows, columns = quant.shape
    levels = quant[...].astype(jnp.float32)
    factors = scales[...].T
    for block in range(columns // BLOCK):
        run = slice(block * BLOCK, (block + 1) * BLOCK)
        weight[:, run] = (levels[:, run] * factors[:, block : block + 1]).astype(weight.dtype)
    part = half.shape[0]
    half[...] = weight[pl.ds(pl.multiple_of(odd[0] * part, part), part), :]


def weights(odd, quant, scales):
    rows, columns = quant.shape
    vmem = pl.BlockSpec(memory_space=pltpu.VMEM)
    quant, scales = (
        pltpu.with_memory_space_constraint(v, pltpu.HBM) for v in (quant, scales.T)
    )
    return pl.pallas_call(
        weight_kernel,
        out_shape=[
            jax.ShapeDtypeStruct((rows, columns), jnp.bfloat16),
            jax.ShapeDtypeStruct((rows // 2, columns), jnp.bfloat16),
        ],
        in_specs=[pl.BlockSpec(memory_space=pltpu.SMEM), vmem, vmem],
        out_specs=[vmem, vmem],
        compiler_params=pltpu.CompilerParams(vmem_limit_bytes=8 * MIB),
        cost_estimate=pl.CostEstimate(
            flops=rows * columns, bytes_accessed=4 * rows * columns, transcendentals=0
        ),
        name="weights",
    )(odd, quant, scales)


def partial_kernel(
    factor, where, acts, acts_in, grads, grads_in, left, r0, r1, r2, r3, *scratch
):
    lhs, rhs, lbuf, rbuf, in_sems, out_sems = scratch
    tokens = acts.shape[0]
    steps = lhs.shape[0]
    each = NY * NZH // steps
    _, _, rows, cut = left.shape
    span = rows * NX
    core, x, y = where[0], where[1], where[2]
    row_group = [lax.rem(k + NX - x, NX) for k in range(NX)]

    first = [
        pltpu.make_async_copy(
            source, rhs.at[pl.ds(half * tokens, tokens)], in_sems.at[2 * NY * NZH + half]
        )
        for half, source in enumerate((grads, grads_in))
    ]
    for copy in first:
        copy.start()
    loads = []
    for j in range(NY * NZH):
        block = j % NZH * NY + lax.rem(y + j // NZH, NY)
        start = pl.multiple_of((block * NC + core) * span, span)
        for half, source in enumerate((acts, acts_in)):
            loads.append(
                pltpu.make_async_copy(
                    source.at[:, pl.ds(start, span)],
                    lhs.at[j // each, pl.ds(half * tokens, tokens), pl.ds(j % each * span, span)],
                    in_sems.at[2 * j + half],
                )
            )
            loads[-1].start()
    for copy in first:
        copy.wait()
    stores = []
    for step in range(steps):
        for copy in loads[2 * each * step : 2 * each * (step + 1)]:
            copy.wait()
        value = lax.dot_general(
            lhs[step], rhs[...], (((0,), (0,)), ((), ())), preferred_element_type=jnp.float32
        )
        value = (value * factor).astype(left.dtype)
        for t in range(each):
            j = step * each + t
            k, z_hi = j // NZH, j % NZH
            for group in range(NX):
                start = t * span + group * rows
                lbuf[j, group] = value[start : start + rows, :cut]
                rbuf[k, row_group[group] * NZH + z_hi] = value[start : start + rows, cut:]
            place = lax.rem(y + k, NY) * NZH + z_hi
            stores.append(
                pltpu.make_async_copy(lbuf.at[j], left.at[:, place], out_sems.at[NY + j])
            )
            stores[-1].start()
            if z_hi == NZH - 1:
                stores.append(
                    pltpu.make_async_copy(rbuf.at[k], (r0, r1, r2, r3)[k], out_sems.at[k])
                )
                stores[-1].start()
    for copy in stores:
        copy.wait()


def partials(where, acts, acts_in, grads, grads_in, factor):
    tokens, width = acts.shape
    columns = grads.shape[1]
    blocks = NZH * NY
    span = width // (blocks * NC)
    rows = span // NX
    steps = 2
    cut = LEFT
    acts, grads = (pltpu.with_memory_space_constraint(v, pltpu.HBM) for v in (acts, grads))
    anywhere = pl.BlockSpec(memory_space=pl.ANY)
    right = (NX * NZH, rows, columns - cut)
    return pl.pallas_call(
        functools.partial(partial_kernel, factor),
        out_shape=[pltpu.HBM((NX, blocks, rows, cut), jnp.bfloat16)]
        + [pltpu.HBM(right, jnp.bfloat16)] * NY,
        in_specs=[pl.BlockSpec(memory_space=pltpu.SMEM)] + [anywhere] * 4,
        out_specs=[anywhere] * (1 + NY),
        scratch_shapes=[
            pltpu.VMEM((steps, 2 * tokens, blocks // steps * span), jnp.bfloat16),
            pltpu.VMEM((2 * tokens, columns), jnp.bfloat16),
            pltpu.VMEM((blocks, NX, rows, cut), jnp.bfloat16),
            pltpu.VMEM((NY, *right), jnp.bfloat16),
            pltpu.SemaphoreType.DMA((2 * blocks + 2,)),
            pltpu.SemaphoreType.DMA((blocks + NY,)),
        ],
        compiler_params=pltpu.CompilerParams(vmem_limit_bytes=24 * MIB),
        cost_estimate=pl.CostEstimate(
            flops=4 * tokens * columns * span * blocks,
            bytes_accessed=2 * blocks * span * columns + 4 * tokens * width,
            transcendentals=0,
        ),
        name="partials",
    )(where, acts, acts_in, grads, grads_in)


def left_kernel(parts, out, held, result, sems, out_sems):
    pieces, terms, rows, columns = held.shape
    stores = []
    copies = [
        pltpu.make_async_copy(parts.at[:, pl.ds(q * rows, rows)], held.at[q], sems.at[q])
        for q in range(pieces)
    ]
    for copy in copies[:AHEAD]:
        copy.start()
    for q, copy in enumerate(copies):
        if q + AHEAD < pieces:
            copies[q + AHEAD].start()
        copy.wait()
        result[q] = total_of([held[q, k] for k in range(terms)], out.dtype)
        stores.append(
            pltpu.make_async_copy(result.at[q], out.at[pl.ds(q * rows, rows)], out_sems.at[q])
        )
        stores[-1].start()
    for copy in stores:
        copy.wait()


def left_sums(parts):
    terms, rows, columns = parts.shape
    pieces = 4
    return pl.pallas_call(
        left_kernel,
        out_shape=pltpu.HBM((rows, columns), parts.dtype),
        in_specs=[pl.BlockSpec(memory_space=pl.ANY)],
        out_specs=pl.BlockSpec(memory_space=pl.ANY),
        scratch_shapes=[
            pltpu.VMEM((pieces, terms, rows // pieces, columns), parts.dtype),
            pltpu.VMEM((pieces, rows // pieces, columns), parts.dtype),
            pltpu.SemaphoreType.DMA((pieces,)),
            pltpu.SemaphoreType.DMA((pieces,)),
        ],
        compiler_params=pltpu.CompilerParams(vmem_limit_bytes=16 * MIB),
        cost_estimate=pl.CostEstimate(
            flops=2 * CHAIN, bytes_accessed=2 * terms * rows * columns, transcendentals=0
        ),
        name="left_sums",
    )(parts)


def right_kernel(*refs):
    held, sems = refs[-2:]
    count = held.shape[0]
    parts, outs = refs[:count], refs[count:-2]
    rows = outs[0].shape[0]
    copies = [
        pltpu.make_async_copy(part, held.at[k], sems.at[k]) for k, part in enumerate(parts)
    ]
    for copy in copies:
        copy.start()
    for copy in copies:
        copy.wait()
    for k, out in enumerate(outs):
        run = slice(k * rows, (k + 1) * rows)
        out[...] = total_of([held[i, run] for i in range(count)], out.dtype)


def right_sums(parts):
    rows, columns = parts[0].shape
    count = len(parts)
    parts = [pltpu.with_memory_space_constraint(parts[0], pltpu.HBM), *parts[1:]]
    return pl.pallas_call(
        right_kernel,
        out_shape=[jax.ShapeDtypeStruct((rows // count, columns), parts[0].dtype)] * count,
        in_specs=[pl.BlockSpec(memory_space=pl.ANY)] * count,
        out_specs=[pl.BlockSpec(memory_space=pltpu.VMEM)] * count,
        scratch_shapes=[
            pltpu.VMEM((count, rows, columns), parts[0].dtype),
            pltpu.SemaphoreType.DMA((count,)),
        ],
        compiler_params=pltpu.CompilerParams(vmem_limit_bytes=16 * MIB),
        cost_estimate=pl.CostEstimate(
            flops=CHAIN, bytes_accessed=2 * count * rows * columns, transcendentals=0
        ),
        name="right_sums",
    )(*parts)


def joined_kernel(left, *refs):
    parts, out = refs[:-1], refs[-1]
    cut = left.shape[2]
    out[:, :cut] = total_of([left[k] for k in range(left.shape[0])], out.dtype)
    out[:, cut:] = total_of([part[...] for part in parts], out.dtype)


def joined_sums(left, parts):
    _, rows, cut = left.shape
    vmem = pl.BlockSpec(memory_space=pltpu.VMEM)
    return pl.pallas_call(
        joined_kernel,
        out_shape=jax.ShapeDtypeStruct((rows, cut + parts[0].shape[1]), left.dtype),
        in_specs=[vmem] * (1 + len(parts)),
        out_specs=vmem,
        compiler_params=pltpu.CompilerParams(vmem_limit_bytes=16 * MIB),
        cost_estimate=pl.CostEstimate(
            flops=CHAIN, bytes_accessed=10 * rows * 1024, transcendentals=0
        ),
        name="joined_sums",
    )(left, *parts)


def input_kernel(where, grads, weight, *rest):
    out, held, lhs, result, in_sems, out_sems = rest[-6:]
    groups, rows, _ = held.shape
    first = pltpu.make_async_copy(grads, lhs, in_sems.at[2 * groups])
    first.start()
    half = rows // 2
    copies = []
    for group in range(groups):
        copies.append(
            [
                pltpu.make_async_copy(
                    weight.at[group, pl.ds(i * half, half)],
                    held.at[group, pl.ds(pl.multiple_of((where[1] ^ i) * half, half), half)],
                    in_sems.at[2 * group + i],
                )
                for i in range(2)
            ]
        )
    for pair in copies[:AHEAD]:
        for copy in pair:
            copy.start()
    first.wait()
    done = []
    for group, pair in enumerate(copies):
        if group + AHEAD < groups:
            for copy in copies[group + AHEAD]:
                copy.start()
        for copy in pair:
            copy.wait()
        run = pl.ds(group * rows, rows)
        result[:, run] = lax.dot_general(
            lhs[...], held[group], (((1,), (1,)), ((), ())), preferred_element_type=jnp.float32
        ).astype(result.dtype)
        start = pl.multiple_of((where[0] + group) * rows, rows)
        done.append(
            pltpu.make_async_copy(
                result.at[:, run], out.at[:, pl.ds(start, rows)], out_sems.at[group]
            )
        )
        done[-1].start()
    for copy in done:
        copy.wait()


def input_part(place, turn, grads, weight, width, before=None):
    tokens, columns = grads.shape
    groups, rows, _ = weight.shape
    weight = pltpu.with_memory_space_constraint(weight, pltpu.HBM)
    args = [jnp.stack([place, turn]).astype(jnp.int32), grads, weight]
    aliases = {}
    if before is not None:
        args.append(before)
        aliases = {3: 0}
    anywhere = pl.BlockSpec(memory_space=pl.ANY)
    return pl.pallas_call(
        input_kernel,
        out_shape=jax.ShapeDtypeStruct((tokens, width), jnp.bfloat16),
        in_specs=[pl.BlockSpec(memory_space=pltpu.SMEM)] + [anywhere] * (len(args) - 1),
        out_specs=anywhere,
        scratch_shapes=[
            pltpu.VMEM((groups, rows, columns), jnp.bfloat16),
            pltpu.VMEM((tokens, columns), jnp.bfloat16),
            pltpu.VMEM((tokens, groups * rows), jnp.bfloat16),
            pltpu.SemaphoreType.DMA((2 * groups + 1,)),
            pltpu.SemaphoreType.DMA((groups,)),
        ],
        input_output_aliases=aliases,
        compiler_params=pltpu.CompilerParams(vmem_limit_bytes=16 * MIB),
        cost_estimate=pl.CostEstimate(
            flops=2 * tokens * columns * groups * rows,
            bytes_accessed=2 * groups * rows * columns + 4 * tokens * columns,
            transcendentals=0,
        ),
        name="input_part",
    )(*args)


def shards(acts, grads_out, quant, scales):
    tokens, width = acts.shape
    columns = grads_out.shape[1]
    shard_rows = quant.shape[0]
    total_tokens = tokens * lax.axis_size(AXES)
    x, zl, zh, y, c = (lax.axis_index(name) for name in AXES)
    odd = zl % 2
    groups = NY * NC
    chunk = NZH * NZL * 8

    acts_in = shift(acts, "c", 1)
    grads_in = shift(grads_out, "c", 1)
    weight, piece = weights(odd[None].astype(jnp.int32), quant, scales)
    own_half = lax.all_gather(weight, ("y", "c"), axis=0, tiled=True)
    fetched = chip_shift(piece, lambda i, z: (i, (z + NZL) % NZ))

    factor = 1.0 / math.sqrt(total_tokens)
    where = jnp.stack([c, x, y]).astype(jnp.int32)
    where, _ = lax.optimization_barrier((where, weight))
    left, *right = partials(where, acts, acts_in, grads_out, grads_in, factor)
    left = lax.all_to_all(left, "x", split_axis=0, concat_axis=0, tiled=True)
    right = [right[0]] + [shift(right[k], "y", k) for k in (2, 1, 3)]

    fetched, _ = lax.optimization_barrier((fetched, right[2]))
    swapped = chip_shift(fetched, lambda i, z: (i, z ^ 1))
    both = jnp.concatenate([fetched, swapped], axis=0)
    both, *_ = lax.optimization_barrier((both, *right))
    other_half = lax.all_gather(both, ("y", "c"), axis=0, tiled=True)

    right = right_sums([part.reshape(NX * chunk, columns - LEFT) for part in right])
    left = left_sums(left.reshape(NX, NY * chunk, LEFT)).reshape(NY, chunk, LEFT)
    left = lax.all_to_all(left, "y", split_axis=0, concat_axis=0, tiled=True)
    right = [right[0]] + [shift(right[k], "x", k) for k in (2, 1, 3)]
    rows = joined_sums(left, right).reshape(NZ, 8, columns)
    grads_later, _ = lax.optimization_barrier((grads_out, rows))
    rows = lax.all_to_all(rows, ("zh", "zl"), split_axis=0, concat_axis=0, tiled=True)
    own_half = own_half.reshape(groups, shard_rows, columns)
    grad_input = input_part(zh * groups, 0 * odd, grads_later, own_half, width)
    other_half = other_half.reshape(groups, shard_rows, columns)
    grad_input = input_part(
        (1 - zh) * groups, odd, grads_later, other_half, width, grad_input
    )
    grad_input, rows = lax.optimization_barrier((grad_input, rows))
    weight_grad = jnp.sum(rows, axis=0, dtype=jnp.float32)
    return (grad_input, weight_grad)


def solution(mesh):
    fine = Mesh(mesh.devices.reshape(NX, NZL, NZH, NY, NC), AXES)
    tokens = P(AXES, None)
    rows = P(("zh", "y", "c"), None)
    return jax.shard_map(
        shards,
        mesh=fine,
        in_specs=(tokens, tokens, rows, rows),
        out_specs=(tokens, P(("zh", "y", "c", "x", "zl"), None)),
        check_vma=False,
    )
```

```python
import functools
import math

import jax
import jax.numpy as jnp
from jax import lax
from jax.experimental import pallas as pl
from jax.experimental.pallas import tpu as pltpu
from jax.sharding import Mesh
from jax.sharding import PartitionSpec as P

BLOCK = 128
NX, NZL, NZH, NY, NC = 4, 8, 2, 4, 2
NZ = NZL * NZH
AXES = ("x", "zl", "zh", "y", "c")
MIB = 1024 * 1024
AHEAD = 3
LEFT = 768
CHAIN = 16 * 10**9


def shift(value, axis, step):
    size = lax.axis_size(axis)
    return lax.ppermute(value, axis, [(i, (i + step) % size) for i in range(size)])


def chip_shift(value, move):
    def index(x, z, y, c):
        return (((x * NZL + z % NZL) * NZH + z // NZL) * NY + y) * NC + c

    pairs = []
    for x in range(NX):
        for z in range(NZ):
            to_x, to_z = move(x, z)
            for y in range(NY):
                for c in range(NC):
                    pairs.append((index(x, z, y, c), index(to_x, to_z, y, c)))
    return lax.ppermute(value, AXES, pairs)


def total_of(parts, dtype):
    total = parts[0].astype(jnp.float32)
    for part in parts[1:]:
        total = total + part.astype(jnp.float32)
    return total.astype(dtype)


def weight_kernel(odd, quant, scales, weight, half):
    rows, columns = quant.shape
    levels = quant[...].astype(jnp.float32)
    factors = scales[...].T
    for block in range(columns // BLOCK):
        run = slice(block * BLOCK, (block + 1) * BLOCK)
        weight[:, run] = (levels[:, run] * factors[:, block : block + 1]).astype(weight.dtype)
    part = half.shape[0]
    half[...] = weight[pl.ds(pl.multiple_of(odd[0] * part, part), part), :]


def weights(odd, quant, scales):
    rows, columns = quant.shape
    vmem = pl.BlockSpec(memory_space=pltpu.VMEM)
    quant, scales = (
        pltpu.with_memory_space_constraint(v, pltpu.HBM) for v in (quant, scales.T)
    )
    return pl.pallas_call(
        weight_kernel,
        out_shape=[
            jax.ShapeDtypeStruct((rows, columns), jnp.bfloat16),
            jax.ShapeDtypeStruct((rows // 2, columns), jnp.bfloat16),
        ],
        in_specs=[pl.BlockSpec(memory_space=pltpu.SMEM), vmem, vmem],
        out_specs=[vmem, vmem],
        compiler_params=pltpu.CompilerParams(vmem_limit_bytes=8 * MIB),
        cost_estimate=pl.CostEstimate(
            flops=rows * columns, bytes_accessed=4 * rows * columns, transcendentals=0
        ),
        name="weights",
    )(odd, quant, scales)


def partial_kernel(
    factor, where, acts, acts_in, grads, grads_in, left, r0, r1, r2, r3, *scratch
):
    lhs, rhs, lbuf, rbuf, in_sems, out_sems = scratch
    tokens = acts.shape[0]
    steps = lhs.shape[0]
    each = NY * NZH // steps
    _, _, rows, cut = left.shape
    span = rows * NX
    core, x, y = where[0], where[1], where[2]
    row_group = [lax.rem(k + NX - x, NX) for k in range(NX)]

    first = [
        pltpu.make_async_copy(
            source, rhs.at[pl.ds(half * tokens, tokens)], in_sems.at[2 * NY * NZH + half]
        )
        for half, source in enumerate((grads, grads_in))
    ]
    for copy in first:
        copy.start()
    loads = []
    for j in range(NY * NZH):
        block = j % NZH * NY + lax.rem(y + j // NZH, NY)
        start = pl.multiple_of((block * NC + core) * span, span)
        for half, source in enumerate((acts, acts_in)):
            loads.append(
                pltpu.make_async_copy(
                    source.at[:, pl.ds(start, span)],
                    lhs.at[j // each, pl.ds(half * tokens, tokens), pl.ds(j % each * span, span)],
                    in_sems.at[2 * j + half],
                )
            )
            loads[-1].start()
    for copy in first:
        copy.wait()
    stores = []
    for step in range(steps):
        for copy in loads[2 * each * step : 2 * each * (step + 1)]:
            copy.wait()
        value = lax.dot_general(
            lhs[step], rhs[...], (((0,), (0,)), ((), ())), preferred_element_type=jnp.float32
        )
        value = (value * factor).astype(left.dtype)
        for t in range(each):
            j = step * each + t
            k, z_hi = j // NZH, j % NZH
            for group in range(NX):
                start = t * span + group * rows
                lbuf[j, group] = value[start : start + rows, :cut]
                rbuf[k, row_group[group] * NZH + z_hi] = value[start : start + rows, cut:]
            place = lax.rem(y + k, NY) * NZH + z_hi
            stores.append(
                pltpu.make_async_copy(lbuf.at[j], left.at[:, place], out_sems.at[NY + j])
            )
            stores[-1].start()
            if z_hi == NZH - 1:
                stores.append(
                    pltpu.make_async_copy(rbuf.at[k], (r0, r1, r2, r3)[k], out_sems.at[k])
                )
                stores[-1].start()
    for copy in stores:
        copy.wait()


def partials(where, acts, acts_in, grads, grads_in, factor):
    tokens, width = acts.shape
    columns = grads.shape[1]
    blocks = NZH * NY
    span = width // (blocks * NC)
    rows = span // NX
    steps = 2
    cut = LEFT
    acts, grads = (pltpu.with_memory_space_constraint(v, pltpu.HBM) for v in (acts, grads))
    anywhere = pl.BlockSpec(memory_space=pl.ANY)
    right = (NX * NZH, rows, columns - cut)
    return pl.pallas_call(
        functools.partial(partial_kernel, factor),
        out_shape=[pltpu.HBM((NX, blocks, rows, cut), jnp.bfloat16)]
        + [pltpu.HBM(right, jnp.bfloat16)] * NY,
        in_specs=[pl.BlockSpec(memory_space=pltpu.SMEM)] + [anywhere] * 4,
        out_specs=[anywhere] * (1 + NY),
        scratch_shapes=[
            pltpu.VMEM((steps, 2 * tokens, blocks // steps * span), jnp.bfloat16),
            pltpu.VMEM((2 * tokens, columns), jnp.bfloat16),
            pltpu.VMEM((blocks, NX, rows, cut), jnp.bfloat16),
            pltpu.VMEM((NY, *right), jnp.bfloat16),
            pltpu.SemaphoreType.DMA((2 * blocks + 2,)),
            pltpu.SemaphoreType.DMA((blocks + NY,)),
        ],
        compiler_params=pltpu.CompilerParams(vmem_limit_bytes=24 * MIB),
        cost_estimate=pl.CostEstimate(
            flops=4 * tokens * columns * span * blocks,
            bytes_accessed=2 * blocks * span * columns + 4 * tokens * width,
            transcendentals=0,
        ),
        name="partials",
    )(where, acts, acts_in, grads, grads_in)


def left_kernel(parts, out, held, result, sems, out_sems):
    pieces, terms, rows, columns = held.shape
    stores = []
    copies = [
        pltpu.make_async_copy(parts.at[:, pl.ds(q * rows, rows)], held.at[q], sems.at[q])
        for q in range(pieces)
    ]
    for copy in copies[:AHEAD]:
        copy.start()
    for q, copy in enumerate(copies):
        if q + AHEAD < pieces:
            copies[q + AHEAD].start()
        copy.wait()
        result[q] = total_of([held[q, k] for k in range(terms)], out.dtype)
        stores.append(
            pltpu.make_async_copy(result.at[q], out.at[pl.ds(q * rows, rows)], out_sems.at[q])
        )
        stores[-1].start()
    for copy in stores:
        copy.wait()


def left_sums(parts):
    terms, rows, columns = parts.shape
    pieces = 4
    return pl.pallas_call(
        left_kernel,
        out_shape=pltpu.HBM((rows, columns), parts.dtype),
        in_specs=[pl.BlockSpec(memory_space=pl.ANY)],
        out_specs=pl.BlockSpec(memory_space=pl.ANY),
        scratch_shapes=[
            pltpu.VMEM((pieces, terms, rows // pieces, columns), parts.dtype),
            pltpu.VMEM((pieces, rows // pieces, columns), parts.dtype),
            pltpu.SemaphoreType.DMA((pieces,)),
            pltpu.SemaphoreType.DMA((pieces,)),
        ],
        compiler_params=pltpu.CompilerParams(vmem_limit_bytes=16 * MIB),
        cost_estimate=pl.CostEstimate(
            flops=CHAIN, bytes_accessed=2 * terms * rows * columns, transcendentals=0
        ),
        name="left_sums",
    )(parts)


def right_kernel(*refs):
    held, sems = refs[-2:]
    count = held.shape[0]
    parts, outs = refs[:count], refs[count:-2]
    rows = outs[0].shape[0]
    copies = [
        pltpu.make_async_copy(part, held.at[k], sems.at[k]) for k, part in enumerate(parts)
    ]
    for copy in copies:
        copy.start()
    for copy in copies:
        copy.wait()
    for k, out in enumerate(outs):
        run = slice(k * rows, (k + 1) * rows)
        out[...] = total_of([held[i, run] for i in range(count)], out.dtype)


def right_sums(parts):
    rows, columns = parts[0].shape
    count = len(parts)
    parts = [pltpu.with_memory_space_constraint(parts[0], pltpu.HBM), *parts[1:]]
    return pl.pallas_call(
        right_kernel,
        out_shape=[jax.ShapeDtypeStruct((rows // count, columns), parts[0].dtype)] * count,
        in_specs=[pl.BlockSpec(memory_space=pl.ANY)] * count,
        out_specs=[pl.BlockSpec(memory_space=pltpu.VMEM)] * count,
        scratch_shapes=[
            pltpu.VMEM((count, rows, columns), parts[0].dtype),
            pltpu.SemaphoreType.DMA((count,)),
        ],
        compiler_params=pltpu.CompilerParams(vmem_limit_bytes=16 * MIB),
        cost_estimate=pl.CostEstimate(
            flops=CHAIN, bytes_accessed=2 * count * rows * columns, transcendentals=0
        ),
        name="right_sums",
    )(*parts)


def joined_kernel(left, *refs):
    parts, out = refs[:-1], refs[-1]
    cut = left.shape[2]
    out[:, :cut] = total_of([left[k] for k in range(left.shape[0])], out.dtype)
    out[:, cut:] = total_of([part[...] for part in parts], out.dtype)


def joined_sums(left, parts):
    _, rows, cut = left.shape
    vmem = pl.BlockSpec(memory_space=pltpu.VMEM)
    return pl.pallas_call(
        joined_kernel,
        out_shape=jax.ShapeDtypeStruct((rows, cut + parts[0].shape[1]), left.dtype),
        in_specs=[vmem] * (1 + len(parts)),
        out_specs=vmem,
        compiler_params=pltpu.CompilerParams(vmem_limit_bytes=16 * MIB),
        cost_estimate=pl.CostEstimate(
            flops=CHAIN, bytes_accessed=10 * rows * 1024, transcendentals=0
        ),
        name="joined_sums",
    )(left, *parts)


def input_kernel(where, grads, weight, *rest):
    out, held, lhs, result, in_sems, out_sems = rest[-6:]
    groups, rows, _ = held.shape
    first = pltpu.make_async_copy(grads, lhs, in_sems.at[2 * groups])
    first.start()
    half = rows // 2
    copies = []
    for group in range(groups):
        copies.append(
            [
                pltpu.make_async_copy(
                    weight.at[group, pl.ds(i * half, half)],
                    held.at[group, pl.ds(pl.multiple_of((where[1] ^ i) * half, half), half)],
                    in_sems.at[2 * group + i],
                )
                for i in range(2)
            ]
        )
    for pair in copies[:AHEAD]:
        for copy in pair:
            copy.start()
    first.wait()
    done = []
    for group, pair in enumerate(copies):
        if group + AHEAD < groups:
            for copy in copies[group + AHEAD]:
                copy.start()
        for copy in pair:
            copy.wait()
        run = pl.ds(group * rows, rows)
        result[:, run] = lax.dot_general(
            lhs[...], held[group], (((1,), (1,)), ((), ())), preferred_element_type=jnp.float32
        ).astype(result.dtype)
        start = pl.multiple_of((where[0] + group) * rows, rows)
        done.append(
            pltpu.make_async_copy(
                result.at[:, run], out.at[:, pl.ds(start, rows)], out_sems.at[group]
            )
        )
        done[-1].start()
    for copy in done:
        copy.wait()


def input_part(place, turn, grads, weight, width, before=None):
    tokens, columns = grads.shape
    groups, rows, _ = weight.shape
    weight = pltpu.with_memory_space_constraint(weight, pltpu.HBM)
    args = [jnp.stack([place, turn]).astype(jnp.int32), grads, weight]
    aliases = {}
    if before is not None:
        args.append(before)
        aliases = {3: 0}
    anywhere = pl.BlockSpec(memory_space=pl.ANY)
    return pl.pallas_call(
        input_kernel,
        out_shape=jax.ShapeDtypeStruct((tokens, width), jnp.bfloat16),
        in_specs=[pl.BlockSpec(memory_space=pltpu.SMEM)] + [anywhere] * (len(args) - 1),
        out_specs=anywhere,
        scratch_shapes=[
            pltpu.VMEM((groups, rows, columns), jnp.bfloat16),
            pltpu.VMEM((tokens, columns), jnp.bfloat16),
            pltpu.VMEM((tokens, groups * rows), jnp.bfloat16),
            pltpu.SemaphoreType.DMA((2 * groups + 1,)),
            pltpu.SemaphoreType.DMA((groups,)),
        ],
        input_output_aliases=aliases,
        compiler_params=pltpu.CompilerParams(vmem_limit_bytes=16 * MIB),
        cost_estimate=pl.CostEstimate(
            flops=2 * tokens * columns * groups * rows,
            bytes_accessed=2 * groups * rows * columns + 4 * tokens * columns,
            transcendentals=0,
        ),
        name="input_part",
    )(*args)


def shards(acts, grads_out, quant, scales):
    tokens, width = acts.shape
    columns = grads_out.shape[1]
    shard_rows = quant.shape[0]
    total_tokens = tokens * lax.axis_size(AXES)
    x, zl, zh, y, c = (lax.axis_index(name) for name in AXES)
    odd = zl % 2
    groups = NY * NC
    chunk = NZH * NZL * 8

    acts_in = shift(acts, "c", 1)
    grads_in = shift(grads_out, "c", 1)
    weight, piece = weights(odd[None].astype(jnp.int32), quant, scales)
    own_half = lax.all_gather(weight, ("y", "c"), axis=0, tiled=True)
    fetched = chip_shift(piece, lambda i, z: (i, (z + NZL) % NZ))

    factor = 1.0 / math.sqrt(total_tokens)
    where = jnp.stack([c, x, y]).astype(jnp.int32)
    where, _ = lax.optimization_barrier((where, weight))
    left, *right = partials(where, acts, acts_in, grads_out, grads_in, factor)
    left = lax.all_to_all(left, "x", split_axis=0, concat_axis=0, tiled=True)
    right = [right[0]] + [shift(right[k], "y", k) for k in (2, 1, 3)]

    swapped = chip_shift(fetched, lambda i, z: (i, z ^ 1))
    both = jnp.concatenate([fetched, swapped], axis=0)
    both, *_ = lax.optimization_barrier((both, right[1], right[3]))
    other_half = lax.all_gather(both, ("y", "c"), axis=0, tiled=True)

    right = right_sums([part.reshape(NX * chunk, columns - LEFT) for part in right])
    left = left_sums(left.reshape(NX, NY * chunk, LEFT)).reshape(NY, chunk, LEFT)
    left = lax.all_to_all(left, "y", split_axis=0, concat_axis=0, tiled=True)
    right = [right[0]] + [shift(right[k], "x", k) for k in (2, 1, 3)]
    rows = joined_sums(left, right).reshape(NZ, 8, columns)
    grads_later, _ = lax.optimization_barrier((grads_out, rows))
    rows = lax.all_to_all(rows, ("zh", "zl"), split_axis=0, concat_axis=0, tiled=True)
    own_half = own_half.reshape(groups, shard_rows, columns)
    grad_input = input_part(zh * groups, 0 * odd, grads_later, own_half, width)
    other_half = other_half.reshape(groups, shard_rows, columns)
    grad_input = input_part(
        (1 - zh) * groups, odd, grads_later, other_half, width, grad_input
    )
    grad_input, rows = lax.optimization_barrier((grad_input, rows))
    weight_grad = jnp.sum(rows, axis=0, dtype=jnp.float32)
    return (grad_input, weight_grad)


def solution(mesh):
    fine = Mesh(mesh.devices.reshape(NX, NZL, NZH, NY, NC), AXES)
    tokens = P(AXES, None)
    rows = P(("zh", "y", "c"), None)
    return jax.shard_map(
        shards,
        mesh=fine,
        in_specs=(tokens, tokens, rows, rows),
        out_specs=(tokens, P(("zh", "y", "c", "x", "zl"), None)),
        check_vma=False,
    )
```
